512 devices in a mesh: grp: 16 (over z_lo, core), dev: 32 (over z_hi, x, y).
Axes of the slice: x: 4, y: 4, z: 16 (z_hi: 2, z_lo: 8; z = z_hi * 8 + z_lo), core: 2. Of those that a mesh axis runs over, the one named last changes fastest.
Arguments:
- embeddings: float32 [131072, 1280], P(('grp', 'dev')), may hold values from -6 to 6
- factor: float32 [131072, 512], P(('grp', 'dev')), may hold values from -0.078125 to 0.078125
- pivots: int32 [512], replicated, may hold values from 0 to 131071, as said below
Outputs:
- new_factor: float32 [131072, 512], P(('grp', 'dev'))
- core_columns: float32 [1024, 512], P('dev')
The draws below stay inside these ranges and needn't reach their ends.
Inputs may be any that keep to these rules, and one draw needn't show every extreme that they name: The pivots are distinct row indices. The rows of one device (256 consecutive rows) hold at most 3 pivots and some device holds exactly 3; the rows of one index of grp hold at most 48 pivots and some index holds exactly 48.
All inputs are finite; a program needn't handle non-finite values.
Results may differ from the reference program's by a relative error of at most 0.00022.
Values sent between devices are 32-bit elements; how exact they have to be, the bound alone decides.
No kernel may reach another device: no remote copies, remote signals or barrier semaphores. Data moves between devices by JAX's collectives and lax.ppermute only.
A program may use at most 128 MiB of HBM per device.

```python
import jax
import jax.numpy as jnp
from jax import lax

D = 1280
K0 = 512
S = 512
ROWS_DEV = 256
TOTAL = 131072
P_MAX = 3
N_GRP = 16
N_DEV = 32


def draw_pivots(key, part):
    key = jax.random.fold_in(key, 7)
    k_grp, k_dev, k_row, k_ord = jax.random.split(key, 4)
    mean_grp = S // N_GRP
    grp_rank = jax.random.permutation(k_grp, N_GRP)
    grp_total = jnp.where(grp_rank % 2 == 0, mean_grp + mean_grp // 2, mean_grp - mean_grp // 2)
    dev_keys = jax.random.split(k_dev, N_GRP)
    dev_rank = jax.vmap(lambda k: jax.random.permutation(k, N_DEV))(dev_keys)
    counts = jnp.clip(grp_total[:, None] - dev_rank * P_MAX, 0, P_MAX).reshape(-1)
    row_keys = jax.random.split(k_row, N_GRP * N_DEV)
    local_rows = jax.vmap(lambda k: jax.random.permutation(k, ROWS_DEV)[:P_MAX])(row_keys)
    devices_all = jnp.arange(N_GRP * N_DEV, dtype=jnp.int32)
    indices = devices_all[:, None] * ROWS_DEV + local_rows.astype(jnp.int32)
    live = jnp.arange(P_MAX)[None, :] < counts[:, None]
    order = jnp.argsort(jnp.where(live, 0, 1).reshape(-1), stable=True)
    chosen = indices.reshape(-1)[order[:S]]
    shuffle = jax.random.permutation(k_ord, S)
    return chosen[shuffle].astype(jnp.int32)


def levels(stream_key, dims, cuts, low, high):
    def one(dim, parts):
        heights = jax.random.uniform(jax.random.fold_in(jax.random.fold_in(stream_key, 6), dim), (parts,), jnp.float32, low / len(cuts), high / len(cuts))
        return jnp.repeat(jnp.exp(heights), dims[dim] // parts).reshape((-1,) + (1,) * (len(dims) - dim - 1))

    factor_of = one(*cuts[0])
    for cut in cuts[1:]:
        factor_of = factor_of * one(*cut)
    return factor_of


def centred(own_key, dims, scale, limit, cuts=(), kind=jnp.bfloat16):
    drawn = scale * jax.random.normal(own_key, dims, jnp.float32)
    if cuts:
        drawn = drawn * levels(own_key, dims, cuts, -0.22, 0.18)
    return jnp.clip(drawn, -limit, limit).astype(kind)


def setup_inputs(seed: int = 0) -> dict:
    seeds = jax.random.split(jax.random.key(seed), 4)
    return {
        "embeddings": centred(seeds[0], (TOTAL, D), 1.0, 6.0, ((0, 512),), jnp.float32),
        "factor": centred(seeds[1], (TOTAL, K0), (10 * K0) ** -0.5, 0.078125, ((0, 512),), jnp.float32),
        "pivots": draw_pivots(jax.random.fold_in(seeds[3], 71), 0),
    }


ridge_term = 1.0
core_ridge = 1.0

def kernel_tile(left, right):
    left_sq = jnp.sum(left * left, axis=1)
    right_sq = jnp.sum(right * right, axis=1)
    cross = jnp.dot(left.astype(jnp.float32), right.T.astype(jnp.float32), precision=lax.Precision.HIGHEST, preferred_element_type=jnp.float32)
    return jnp.exp(-(left_sq[:, None] + right_sq[None, :] - 2.0 * cross) / (2.0 * D))

def reference(embeddings, factor, pivots):
    chosen = jnp.take(embeddings, pivots, axis=0)
    chosen_factor = jnp.take(factor, pivots, axis=0)
    pivot_block = kernel_tile(chosen, chosen) - jnp.dot(chosen_factor.astype(jnp.float32), chosen_factor.T.astype(jnp.float32), precision=lax.Precision.HIGHEST, preferred_element_type=jnp.float32)
    pivot_block = pivot_block + ridge_term * jnp.eye(S, dtype=jnp.float32)
    lower = jnp.linalg.cholesky(pivot_block)
    residual_tile = kernel_tile(embeddings, chosen) - jnp.dot(factor.astype(jnp.float32), chosen_factor.T.astype(jnp.float32), precision=lax.Precision.HIGHEST, preferred_element_type=jnp.float32)
    new_factor = lax.linalg.triangular_solve(lower, residual_tile, left_side=False, lower=True, transpose_a=True)
    full_factor = jnp.concatenate([factor, new_factor], axis=1)
    core_columns = jnp.dot(full_factor.T.astype(jnp.float32), new_factor.astype(jnp.float32), precision=lax.Precision.HIGHEST, preferred_element_type=jnp.float32)
    shifted = jnp.concatenate([jnp.zeros((K0, S), jnp.float32), jnp.eye(S, dtype=jnp.float32)], axis=0)
    return (new_factor, core_columns + core_ridge * shifted)
```

```python
import functools

import jax
import jax.numpy as jnp
from jax import lax
from jax.experimental import pallas as pl
from jax.experimental.pallas import tpu as pltpu
from jax.sharding import Mesh
from jax.sharding import PartitionSpec as P

ridge_term = 1.0
core_ridge = 1.0

SLOTS = 3
BLOCK = 128
PANEL = 8
f32 = jnp.float32
bf16 = jnp.bfloat16


def split2(a):
    high = a.astype(bf16)
    return high, (a - high.astype(f32)).astype(bf16)


def split3(a):
    high = a.astype(bf16)
    rest = a - high.astype(f32)
    mid = rest.astype(bf16)
    return high, mid, (rest - mid.astype(f32)).astype(bf16)


def mul(a, b, dims):
    return lax.dot_general(a, b, (dims, ((), ())), preferred_element_type=f32)


def mul3(a, b, dims):
    (ah, al), (bh, bl) = a, b
    return mul(ah, bh, dims) + (mul(ah, bl, dims) + mul(al, bh, dims))


NN = ((1,), (0,))
NT = ((1,), (1,))
TN = ((0,), (0,))


def pick_kernel(width, place_ref, pivots_ref, emb_ref, fac_ref, out_ref):
    base, core = place_ref[0], place_ref[1]
    rows_dev = emb_ref.shape[0]
    count = pivots_ref.shape[1]
    local = (pivots_ref[...] - base).astype(f32)
    order = lax.broadcasted_iota(jnp.int32, (1, count), 1).astype(f32)
    inside = jnp.where((local >= 0) & (local < rows_dev), 1.0, 0.0)
    sub = lax.broadcasted_iota(jnp.int32, (8, rows_dev), 0)
    lane = lax.broadcasted_iota(jnp.int32, (8, rows_dev), 1).astype(f32)
    sub_tag = lax.broadcasted_iota(jnp.int32, (8, BLOCK), 0)
    hot = jnp.zeros((8, rows_dev), f32)
    tag = jnp.full((8, BLOCK), -1.0, f32)
    for k in range(SLOTS):
        pos = jnp.min(jnp.where(inside > 0, order, float(count)), axis=1, keepdims=True)
        hit = order == pos
        row = jnp.sum(jnp.where(hit, local, 0.0), axis=1, keepdims=True)
        valid = pos < count
        row = jnp.where(valid, row, -1.0)
        hot = hot + jnp.where((sub == k) & (lane == row), 1.0, 0.0)
        tag = jnp.where((sub_tag == k), jnp.where(valid, pos, -1.0), tag)
        inside = jnp.where(hit, 0.0, inside)
    hot = hot.astype(bf16)
    pieces = []
    for ref in (emb_ref, fac_ref):
        for c in range(0, ref.shape[1], 256):
            high, mid, low = split3(ref[:, c : c + 256])
            pieces.append(mul(hot, high, NN) + (mul(hot, mid, NN) + mul(hot, low, NN)))
    rows = jnp.concatenate(pieces + [jnp.zeros((8, BLOCK), f32)], axis=1)
    lane_out = lax.broadcasted_iota(jnp.int32, (8, BLOCK), 1)
    for j in range(out_ref.shape[0]):
        first = width * j
        tile = first // BLOCK * BLOCK
        window = rows[:, tile : tile + 2 * BLOCK]
        if first > tile:
            window = pltpu.roll(window, 2 * BLOCK - (first - tile), 1)
        piece = jnp.where(lane_out < width, window[:, :BLOCK], jnp.where(lane_out == width, tag, 0.0))
        piece = jnp.where(core == 0, piece, pltpu.roll(piece, BLOCK // 2, 1))
        out_ref[j] = piece


def select_kernel(width, slots_ref, out_ref):
    slots = slots_ref[...]
    count = out_ref.shape[1]
    order = lax.broadcasted_iota(jnp.int32, (1, count), 1).astype(f32)
    half = BLOCK // 2
    parts = split3(slots)
    total = None
    for c in range(2):
        tag = slots[:, c * half + width : c * half + width + 1]
        hot = jnp.where(tag == order, 1.0, 0.0).astype(bf16)
        for part in parts:
            got = mul(part, hot, TN)[c * half : c * half + width]
            total = got if total is None else total + got
    out_ref[...] = total


def factor_block(mat_ref, off, inv_ref, d_ref, e_ref):
    d_ref[...] = mat_ref[pl.ds(off, BLOCK), pl.ds(off, BLOCK)]
    e_ref[...] = jnp.where(
        lax.broadcasted_iota(jnp.int32, (BLOCK, BLOCK), 0)
        == lax.broadcasted_iota(jnp.int32, (BLOCK, BLOCK), 1),
        1.0,
        0.0,
    ).astype(f32)
    full = (PANEL, BLOCK)

    def spread(a, lane):
        return jnp.broadcast_to(a[:, lane : lane + 1], full)

    for p in range(BLOCK // PANEL):
        first = p * PANEL
        rows = [jnp.broadcast_to(d_ref[first + k : first + k + 1, :], full) for k in range(PANEL)]
        invs = [jnp.broadcast_to(e_ref[first + k : first + k + 1, :], full) for k in range(PANEL)]
        s = [[spread(rows[i], first + k) for k in range(i + 1)] for i in range(PANEL)]
        scale = []
        for k in range(PANEL):
            r = lax.rsqrt(s[k][k])
            scale.append(r)
            for i in range(k + 1, PANEL):
                s[i][k] = s[i][k] * r
            for i in range(k + 1, PANEL):
                for j in range(k + 1, i + 1):
                    s[i][j] = s[i][j] - s[i][k] * s[j][k]
        for k in range(PANEL):
            for m in range(k):
                rows[k] = rows[k] - s[k][m] * rows[m]
                invs[k] = invs[k] - s[k][m] * invs[m]
            rows[k] = rows[k] * scale[k]
            invs[k] = invs[k] * scale[k]
            inv_ref[first + k : first + k + 1, :] = invs[k][0:1, :]
        for b in range(p + 1, BLOCK // PANEL):
            at = slice(b * PANEL, (b + 1) * PANEL)
            d = d_ref[at, :]
            e = e_ref[at, :]
            cols = [spread(d, first + k) for k in range(PANEL)]
            for k in range(PANEL):
                for m in range(k):
                    cols[k] = cols[k] - s[k][m] * cols[m]
                cols[k] = cols[k] * scale[k]
            for k in range(PANEL):
                d = d - cols[k] * rows[k]
                e = e - cols[k] * invs[k]
            d_ref[at, :] = d
            e_ref[at, :] = e


def main_kernel(
    place_ref, emb_ref, fac_ref, own_ref, other_ref, new_ref, keep_ref, send_ref,
    ch_ref, cl_ref, sq_ref, mat_ref, inv_ref, d_ref, e_ref, sum_ref,
):
    core = place_ref[1]
    rows_dev, width = emb_ref.shape
    old_rank = fac_ref.shape[1]
    half, count = own_ref.shape
    total = 2 * half
    second = width - half
    scale = 1.0 / (2.0 * width)

    def take(ref, which):
        start = pl.multiple_of(which * half, BLOCK)
        sq = jnp.zeros((1, count), f32)
        for r in range(0, half, BLOCK):
            a = ref[r : r + BLOCK, :]
            high, low = split2(a)
            at = pl.ds(pl.multiple_of(start + r, BLOCK), BLOCK)
            ch_ref[at, :] = high
            cl_ref[at, :] = low
            part = jnp.sum(a * a, axis=0, keepdims=True)
            if r >= second:
                part = jnp.where(which == 0, part, 0.0)
            sq = sq + part
        return sq

    sq = take(own_ref, core) + take(other_ref, 1 - core)
    sq_ref[...] = jnp.transpose(jnp.broadcast_to(sq, (BLOCK, count)))

    def wide(lo, hi):
        return ch_ref[lo:hi, :], cl_ref[lo:hi, :]

    for i in range(count // BLOCK):
        at = slice(i * BLOCK, (i + 1) * BLOCK)
        cross = mul3((ch_ref[:width, at], cl_ref[:width, at]), wide(0, width), TN)
        old = mul3((ch_ref[width:, at], cl_ref[width:, at]), wide(width, total), TN)
        left = sq_ref[at, 0:1]
        block = jnp.exp((2.0 * cross - (left + sq)) * scale) - old
        row = lax.broadcasted_iota(jnp.int32, (BLOCK, count), 0) + i * BLOCK
        col = lax.broadcasted_iota(jnp.int32, (BLOCK, count), 1)
        mat_ref[at, :] = block + jnp.where(row == col, ridge_term, 0.0)
    for i in range(rows_dev // BLOCK):
        at = slice(i * BLOCK, (i + 1) * BLOCK)
        a = emb_ref[at, :]
        cross = mul3(split2(a), wide(0, width), NN)
        old = mul3(split2(fac_ref[at, :]), wide(width, total), NN)
        left = jnp.sum(a * a, axis=1, keepdims=True)
        mat_ref[count + i * BLOCK : count + (i + 1) * BLOCK, :] = (
            jnp.exp((2.0 * cross - (left + sq)) * scale) - old
        )

    all_rows = count + rows_dev

    def step(kb, carry):
        off = pl.multiple_of(kb * BLOCK, BLOCK)
        factor_block(mat_ref, off, inv_ref, d_ref, e_ref)
        panel = mul3(split2(mat_ref[:, pl.ds(off, BLOCK)]), split2(inv_ref[...]), NT)
        new_ref[:, pl.ds(off, BLOCK)] = panel[count:]
        row = lax.broadcasted_iota(jnp.int32, (all_rows, BLOCK), 0)
        panel = jnp.where(row >= off + BLOCK, panel, 0.0)
        high, low = split2(panel)
        for r in range(0, all_rows, 256):
            mat_ref[r : r + 256, :] = mat_ref[r : r + 256, :] - mul3(
                (high[r : r + 256], low[r : r + 256]), (high[:count], low[:count]), NT
            )
        return carry

    lax.fori_loop(0, count // BLOCK, step, 0)

    new = split2(new_ref[...])
    for i in range(old_rank // BLOCK):
        at = slice(i * BLOCK, (i + 1) * BLOCK)
        sum_ref[at, :] = mul3(split2(fac_ref[:, at]), new, TN)
    for i in range(count // BLOCK):
        at = slice(i * BLOCK, (i + 1) * BLOCK)
        sum_ref[old_rank + i * BLOCK : old_rank + (i + 1) * BLOCK, :] = mul3(
            (new[0][:, at], new[1][:, at]), new, TN
        )
    _, n_zh, part, _ = keep_ref.shape
    shares = keep_ref.shape[0]
    for zh in range(n_zh):
        for j in range(shares):
            start = (zh * shares + j) * 2 * part
            keep_ref[j, zh] = sum_ref[pl.ds(pl.multiple_of(start + core * part, part), part), :]
            send_ref[j, zh] = sum_ref[pl.ds(pl.multiple_of(start + (1 - core) * part, part), part), :]


VMEM = pl.BlockSpec(memory_space=pltpu.VMEM)
SMEM = pl.BlockSpec(memory_space=pltpu.SMEM)
PARAMS = pltpu.CompilerParams(vmem_limit_bytes=48 * 1024 * 1024)


def on_device(n_xy, n_z, embeddings, factor, pivots):
    rows_dev, width = embeddings.shape
    old_rank = factor.shape[1]
    count = pivots.shape[0]
    total = width + old_rank
    slices = 2 * n_xy
    piece = total // slices
    core = lax.axis_index("core")
    mine = lax.axis_index(("zl", "core", "zh", "x", "y"))
    place = jnp.stack([mine * rows_dev, core]).astype(jnp.int32)
    sent = pl.pallas_call(
        functools.partial(pick_kernel, piece),
        out_shape=jax.ShapeDtypeStruct((slices, 8, BLOCK), f32),
        in_specs=[SMEM, VMEM, VMEM, VMEM],
        out_specs=VMEM,
        compiler_params=PARAMS,
        name="pick",
    )(place, pivots.reshape(1, count), embeddings, factor)
    got = lax.all_to_all(sent, ("core", "x", "y"), 0, 0, tiled=True)
    packed = (got[:n_xy] + got[n_xy:])[:, :SLOTS].reshape(n_xy * SLOTS, BLOCK)
    packed = jnp.broadcast_to(packed[None], (n_z, n_xy * SLOTS, BLOCK))
    slots = lax.all_to_all(packed, ("zl", "zh"), 0, 0, tiled=True)
    chosen_slice = pl.pallas_call(
        functools.partial(select_kernel, piece),
        out_shape=jax.ShapeDtypeStruct((piece, count), f32),
        in_specs=[VMEM],
        out_specs=VMEM,
        compiler_params=PARAMS,
        name="select",
    )(slots.reshape(n_z * n_xy * SLOTS, BLOCK))
    wide = jnp.broadcast_to(chosen_slice[None], (n_xy, piece, count))
    own = lax.all_to_all(wide, ("x", "y"), 0, 0, tiled=True).reshape(n_xy * piece, count)
    other = lax.ppermute(own, "core", [(0, 1), (1, 0)])
    share = (old_rank + count) // slices
    part = share // 2
    split = jax.ShapeDtypeStruct((n_xy, 2, part, count), f32)
    new_factor, keep, send = pl.pallas_call(
        main_kernel,
        out_shape=(jax.ShapeDtypeStruct((rows_dev, count), f32), split, split),
        in_specs=[SMEM, VMEM, VMEM, VMEM, VMEM],
        out_specs=(VMEM, VMEM, VMEM),
        scratch_shapes=[
            pltpu.VMEM((total, count), bf16),
            pltpu.VMEM((total, count), bf16),
            pltpu.VMEM((count, BLOCK), f32),
            pltpu.VMEM((count + rows_dev, count), f32),
            pltpu.VMEM((BLOCK, BLOCK), f32),
            pltpu.VMEM((BLOCK, BLOCK), f32),
            pltpu.VMEM((BLOCK, BLOCK), f32),
            pltpu.VMEM((old_rank + count, count), f32),
        ],
        compiler_params=PARAMS,
        name="main",
    )(place, embeddings, factor, own, other)
    pair = keep + lax.ppermute(send, "core", [(0, 1), (1, 0)])
    layer = jnp.sum(lax.all_to_all(pair, ("x", "y"), 0, 0, tiled=True), axis=0)
    spread = jnp.broadcast_to(layer[None], (n_z // 2, 2, part, count)).reshape(n_z, part, count)
    summed = jnp.sum(lax.all_to_all(spread, ("zl", "zh"), 0, 0, tiled=True), axis=0)
    core_share = lax.all_gather(summed, "core", axis=0, tiled=True)
    my_dev = lax.axis_index(("zh", "x", "y"))
    global_rows = my_dev * share + jnp.arange(share)
    diagonal_hit = global_rows[:, None] - old_rank == jnp.arange(count)[None, :]
    return new_factor, core_share + core_ridge * diagonal_hit.astype(f32)


def solution(mesh):
    n_zl, n_zh, n_x = 8, 2, 4
    n_y = mesh.shape["dev"] // (n_zh * n_x)
    n_core = mesh.shape["grp"] // n_zl
    axes = ("zl", "core", "zh", "x", "y")
    fine = Mesh(mesh.devices.reshape(n_zl, n_core, n_zh, n_x, n_y), axes)
    in_specs = (P(axes, None), P(axes, None), P())
    out_specs = (P(axes, None), P(("zh", "x", "y"), None))
    return jax.shard_map(
        functools.partial(on_device, n_x * n_y, n_zl * n_zh),
        mesh=fine, in_specs=in_specs, out_specs=out_specs, check_vma=False,
    )
```

```python
import functools

import jax
import jax.numpy as jnp
from jax import lax
from jax.experimental import pallas as pl
from jax.experimental.pallas import tpu as pltpu
from jax.sharding import Mesh
from jax.sharding import PartitionSpec as P

ridge_term = 1.0
core_ridge = 1.0

SLOTS = 3
BLOCK = 128
PANEL = 8
f32 = jnp.float32
bf16 = jnp.bfloat16


def split2(a):
    high = a.astype(bf16)
    return high, (a - high.astype(f32)).astype(bf16)


def split3(a):
    high = a.astype(bf16)
    rest = a - high.astype(f32)
    mid = rest.astype(bf16)
    return high, mid, (rest - mid.astype(f32)).astype(bf16)


def mul(a, b, dims):
    return lax.dot_general(a, b, (dims, ((), ())), preferred_element_type=f32)


def mul3(a, b, dims):
    (ah, al), (bh, bl) = a, b
    return mul(ah, bh, dims) + (mul(ah, bl, dims) + mul(al, bh, dims))


NN = ((1,), (0,))
NT = ((1,), (1,))
TN = ((0,), (0,))


def pick_kernel(width, place_ref, pivots_ref, emb_ref, fac_ref, out_ref):
    base, core = place_ref[0], place_ref[1]
    rows_dev = emb_ref.shape[0]
    count = pivots_ref.shape[1]
    local = (pivots_ref[...] - base).astype(f32)
    order = lax.broadcasted_iota(jnp.int32, (1, count), 1).astype(f32)
    inside = jnp.where((local >= 0) & (local < rows_dev), 1.0, 0.0)
    sub = lax.broadcasted_iota(jnp.int32, (8, rows_dev), 0)
    lane = lax.broadcasted_iota(jnp.int32, (8, rows_dev), 1).astype(f32)
    sub_tag = lax.broadcasted_iota(jnp.int32, (8, BLOCK), 0)
    hot = jnp.zeros((8, rows_dev), f32)
    tag = jnp.full((8, BLOCK), -1.0, f32)
    for k in range(SLOTS):
        pos = jnp.min(jnp.where(inside > 0, order, float(count)), axis=1, keepdims=True)
        hit = order == pos
        row = jnp.sum(jnp.where(hit, local, 0.0), axis=1, keepdims=True)
        valid = pos < count
        row = jnp.where(valid, row, -1.0)
        hot = hot + jnp.where((sub == k) & (lane == row), 1.0, 0.0)
        tag = jnp.where((sub_tag == k), jnp.where(valid, pos, -1.0), tag)
        inside = jnp.where(hit, 0.0, inside)
    hot = hot.astype(bf16)
    pieces = []
    for ref in (emb_ref, fac_ref):
        for c in range(0, ref.shape[1], 256):
            high, mid, low = split3(ref[:, c : c + 256])
            pieces.append(mul(hot, high, NN) + (mul(hot, mid, NN) + mul(hot, low, NN)))
    rows = jnp.concatenate(pieces + [jnp.zeros((8, BLOCK), f32)], axis=1)
    lane_out = lax.broadcasted_iota(jnp.int32, (8, BLOCK), 1)
    for j in range(out_ref.shape[0]):
        first = width * j
        tile = first // BLOCK * BLOCK
        window = rows[:, tile : tile + 2 * BLOCK]
        if first > tile:
            window = pltpu.roll(window, 2 * BLOCK - (first - tile), 1)
        piece = jnp.where(lane_out < width, window[:, :BLOCK], jnp.where(lane_out == width, tag, 0.0))
        piece = jnp.where(core == 0, piece, pltpu.roll(piece, BLOCK // 2, 1))
        out_ref[j] = piece


def select_kernel(width, slots_ref, out_ref):
    slots = slots_ref[...]
    count = out_ref.shape[1]
    order = lax.broadcasted_iota(jnp.int32, (1, count), 1).astype(f32)
    half = BLOCK // 2
    parts = split3(slots)
    total = None
    for c in range(2):
        tag = slots[:, c * half + width : c * half + width + 1]
        hot = jnp.where(tag == order, 1.0, 0.0).astype(bf16)
        for part in parts:
            got = mul(part, hot, TN)[c * half : c * half + width]
            total = got if total is None else total + got
    out_ref[...] = total


def factor_block(mat_ref, off, inv_ref, d_ref, e_ref):
    d_ref[...] = mat_ref[pl.ds(off, BLOCK), pl.ds(off, BLOCK)]
    e_ref[...] = jnp.where(
        lax.broadcasted_iota(jnp.int32, (BLOCK, BLOCK), 0)
        == lax.broadcasted_iota(jnp.int32, (BLOCK, BLOCK), 1),
        1.0,
        0.0,
    ).astype(f32)
    full = (PANEL, BLOCK)

    def spread(a, lane):
        return jnp.broadcast_to(a[:, lane : lane + 1], full)

    for p in range(BLOCK // PANEL):
        first = p * PANEL
        rows = [jnp.broadcast_to(d_ref[first + k : first + k + 1, :], full) for k in range(PANEL)]
        invs = [jnp.broadcast_to(e_ref[first + k : first + k + 1, :], full) for k in range(PANEL)]
        s = [[spread(rows[i], first + k) for k in range(i + 1)] for i in range(PANEL)]
        scale = []
        for k in range(PANEL):
            r = lax.rsqrt(s[k][k])
            scale.append(r)
            for i in range(k + 1, PANEL):
                s[i][k] = s[i][k] * r
            for i in range(k + 1, PANEL):
                for j in range(k + 1, i + 1):
                    s[i][j] = s[i][j] - s[i][k] * s[j][k]
        for k in range(PANEL):
            for m in range(k):
                rows[k] = rows[k] - s[k][m] * rows[m]
                invs[k] = invs[k] - s[k][m] * invs[m]
            rows[k] = rows[k] * scale[k]
            invs[k] = invs[k] * scale[k]
            inv_ref[first + k : first + k + 1, :] = invs[k][0:1, :]
        for b in range(p + 1, BLOCK // PANEL):
            at = slice(b * PANEL, (b + 1) * PANEL)
            d = d_ref[at, :]
            e = e_ref[at, :]
            cols = [spread(d, first + k) for k in range(PANEL)]
            for k in range(PANEL):
                for m in range(k):
                    cols[k] = cols[k] - s[k][m] * cols[m]
                cols[k] = cols[k] * scale[k]
            for k in range(PANEL):
                d = d - cols[k] * rows[k]
                e = e - cols[k] * invs[k]
            d_ref[at, :] = d
            e_ref[at, :] = e


def main_kernel(
    place_ref, emb_ref, fac_ref, own_ref, other_ref, new_ref, keep_ref, send_ref,
    ch_ref, cl_ref, sq_ref, mat_ref, inv_ref, d_ref, e_ref, sum_ref,
):
    core = place_ref[1]
    rows_dev, width = emb_ref.shape
    old_rank = fac_ref.shape[1]
    half, count = own_ref.shape
    total = 2 * half
    second = width - half
    scale = 1.0 / (2.0 * width)

    def take(ref, which):
        start = pl.multiple_of(which * half, BLOCK)
        sq = jnp.zeros((1, count), f32)
        for r in range(0, half, BLOCK):
            a = ref[r : r + BLOCK, :]
            high, low = split2(a)
            at = pl.ds(pl.multiple_of(start + r, BLOCK), BLOCK)
            ch_ref[at, :] = high
            cl_ref[at, :] = low
            part = jnp.sum(a * a, axis=0, keepdims=True)
            if r >= second:
                part = jnp.where(which == 0, part, 0.0)
            sq = sq + part
        return sq

    sq = take(own_ref, core) + take(other_ref, 1 - core)
    sq_ref[...] = jnp.transpose(jnp.broadcast_to(sq, (BLOCK, count)))

    def wide(lo, hi, need):
        return ch_ref[lo:hi, :need], cl_ref[lo:hi, :need]

    for i in range(count // BLOCK):
        at = slice(i * BLOCK, (i + 1) * BLOCK)
        need = (i // 2 + 1) * 2 * BLOCK
        cross = mul3((ch_ref[:width, at], cl_ref[:width, at]), wide(0, width, need), TN)
        old = mul3((ch_ref[width:, at], cl_ref[width:, at]), wide(width, total, need), TN)
        left = sq_ref[at, 0:1]
        block = jnp.exp((2.0 * cross - (left + sq[:, :need])) * scale) - old
        row = lax.broadcasted_iota(jnp.int32, (BLOCK, need), 0) + i * BLOCK
        col = lax.broadcasted_iota(jnp.int32, (BLOCK, need), 1)
        mat_ref[at, :need] = block + jnp.where(row == col, ridge_term, 0.0)
    for i in range(rows_dev // BLOCK):
        at = slice(i * BLOCK, (i + 1) * BLOCK)
        a = emb_ref[at, :]
        cross = mul3(split2(a), wide(0, width, count), NN)
        old = mul3(split2(fac_ref[at, :]), wide(width, total, count), NN)
        left = jnp.sum(a * a, axis=1, keepdims=True)
        mat_ref[count + i * BLOCK : count + (i + 1) * BLOCK, :] = (
            jnp.exp((2.0 * cross - (left + sq)) * scale) - old
        )

    all_rows = count + rows_dev

    def step(kb, carry):
        off = pl.multiple_of(kb * BLOCK, BLOCK)
        factor_block(mat_ref, off, inv_ref, d_ref, e_ref)
        panel = mul3(split2(mat_ref[:, pl.ds(off, BLOCK)]), split2(inv_ref[...]), NT)
        new_ref[:, pl.ds(off, BLOCK)] = panel[count:]
        row = lax.broadcasted_iota(jnp.int32, (all_rows, BLOCK), 0)
        panel = jnp.where(row >= off + BLOCK, panel, 0.0)
        high, low = split2(panel)
        for r in range(0, all_rows, 256):
            for c in range(0, min(r + 256, count), 256):

                @pl.when(off + BLOCK < min(r, c) + 256)
                def _():
                    mat_ref[r : r + 256, c : c + 256] = mat_ref[r : r + 256, c : c + 256] - mul3(
                        (high[r : r + 256], low[r : r + 256]), (high[c : c + 256], low[c : c + 256]), NT
                    )

        return carry

    lax.fori_loop(0, count // BLOCK, step, 0)

    new = split2(new_ref[...])
    for i in range(old_rank // BLOCK):
        at = slice(i * BLOCK, (i + 1) * BLOCK)
        sum_ref[at, :] = mul3(split2(fac_ref[:, at]), new, TN)
    for i in range(count // BLOCK):
        at = slice(i * BLOCK, (i + 1) * BLOCK)
        sum_ref[old_rank + i * BLOCK : old_rank + (i + 1) * BLOCK, :] = mul3(
            (new[0][:, at], new[1][:, at]), new, TN
        )
    _, n_zh, part, _ = keep_ref.shape
    shares = keep_ref.shape[0]
    for zh in range(n_zh):
        for j in range(shares):
            start = (zh * shares + j) * 2 * part
            keep_ref[j, zh] = sum_ref[pl.ds(pl.multiple_of(start + core * part, part), part), :]
            send_ref[j, zh] = sum_ref[pl.ds(pl.multiple_of(start + (1 - core) * part, part), part), :]


VMEM = pl.BlockSpec(memory_space=pltpu.VMEM)
SMEM = pl.BlockSpec(memory_space=pltpu.SMEM)
PARAMS = pltpu.CompilerParams(vmem_limit_bytes=48 * 1024 * 1024)


def on_device(n_xy, n_z, embeddings, factor, pivots):
    rows_dev, width = embeddings.shape
    old_rank = factor.shape[1]
    count = pivots.shape[0]
    total = width + old_rank
    slices = 2 * n_xy
    piece = total // slices
    core = lax.axis_index("core")
    mine = lax.axis_index(("zl", "core", "zh", "x", "y"))
    place = jnp.stack([mine * rows_dev, core]).astype(jnp.int32)
    sent = pl.pallas_call(
        functools.partial(pick_kernel, piece),
        out_shape=jax.ShapeDtypeStruct((slices, 8, BLOCK), f32),
        in_specs=[SMEM, VMEM, VMEM, VMEM],
        out_specs=VMEM,
        compiler_params=PARAMS,
        name="pick",
    )(place, pivots.reshape(1, count), embeddings, factor)
    got = lax.all_to_all(sent, ("core", "x", "y"), 0, 0, tiled=True)
    packed = (got[:n_xy] + got[n_xy:])[:, :SLOTS].reshape(n_xy * SLOTS, BLOCK)
    packed = jnp.broadcast_to(packed[None], (n_z, n_xy * SLOTS, BLOCK))
    slots = lax.all_to_all(packed, ("zl", "zh"), 0, 0, tiled=True)
    chosen_slice = pl.pallas_call(
        functools.partial(select_kernel, piece),
        out_shape=jax.ShapeDtypeStruct((piece, count), f32),
        in_specs=[VMEM],
        out_specs=VMEM,
        compiler_params=PARAMS,
        name="select",
    )(slots.reshape(n_z * n_xy * SLOTS, BLOCK))
    wide = jnp.broadcast_to(chosen_slice[None], (n_xy, piece, count))
    own = lax.all_to_all(wide, ("x", "y"), 0, 0, tiled=True).reshape(n_xy * piece, count)
    other = lax.ppermute(own, "core", [(0, 1), (1, 0)])
    share = (old_rank + count) // slices
    part = share // 2
    split = jax.ShapeDtypeStruct((n_xy, 2, part, count), f32)
    new_factor, keep, send = pl.pallas_call(
        main_kernel,
        out_shape=(jax.ShapeDtypeStruct((rows_dev, count), f32), split, split),
        in_specs=[SMEM, VMEM, VMEM, VMEM, VMEM],
        out_specs=(VMEM, VMEM, VMEM),
        scratch_shapes=[
            pltpu.VMEM((total, count), bf16),
            pltpu.VMEM((total, count), bf16),
            pltpu.VMEM((count, BLOCK), f32),
            pltpu.VMEM((count + rows_dev, count), f32),
            pltpu.VMEM((BLOCK, BLOCK), f32),
            pltpu.VMEM((BLOCK, BLOCK), f32),
            pltpu.VMEM((BLOCK, BLOCK), f32),
            pltpu.VMEM((old_rank + count, count), f32),
        ],
        compiler_params=PARAMS,
        name="main",
    )(place, embeddings, factor, own, other)
    pair = keep + lax.ppermute(send, "core", [(0, 1), (1, 0)])
    layer = jnp.sum(lax.all_to_all(pair, ("x", "y"), 0, 0, tiled=True), axis=0)
    n_zl = n_z // 2
    few = part // n_zl
    spread = jnp.swapaxes(layer.reshape(2, n_zl, few, count), 0, 1).reshape(n_z, few, count)
    summed = jnp.sum(lax.all_to_all(spread, ("zl", "zh"), 0, 0, tiled=True), axis=0)
    line = jnp.broadcast_to(summed[None], (n_zl, few, count))
    line = lax.all_to_all(line, "zl", 0, 0, tiled=True).reshape(part, count)
    core_share = lax.all_gather(line, "core", axis=0, tiled=True)
    my_dev = lax.axis_index(("zh", "x", "y"))
    global_rows = my_dev * share + jnp.arange(share)
    diagonal_hit = global_rows[:, None] - old_rank == jnp.arange(count)[None, :]
    return new_factor, core_share + core_ridge * diagonal_hit.astype(f32)


def solution(mesh):
    n_zl, n_zh, n_x = 8, 2, 4
    n_y = mesh.shape["dev"] // (n_zh * n_x)
    n_core = mesh.shape["grp"] // n_zl
    axes = ("zl", "core", "zh", "x", "y")
    fine = Mesh(mesh.devices.reshape(n_zl, n_core, n_zh, n_x, n_y), axes)
    in_specs = (P(axes, None), P(axes, None), P())
    out_specs = (P(axes, None), P(("zh", "x", "y"), None))
    return jax.shard_map(
        functools.partial(on_device, n_x * n_y, n_zl * n_zh),
        mesh=fine, in_specs=in_specs, out_specs=out_specs, check_vma=False,
    )
```

```python
import functools

import jax
import jax.numpy as jnp
from jax import lax
from jax.experimental import pallas as pl
from jax.experimental.pallas import tpu as pltpu
from jax.sharding import Mesh
from jax.sharding import PartitionSpec as P

ridge_term = 1.0
core_ridge = 1.0

SLOTS = 3
BLOCK = 128
PANEL = 8
f32 = jnp.float32
bf16 = jnp.bfloat16


def split2(a):
    high = a.astype(bf16)
    return high, (a - high.astype(f32)).astype(bf16)


def split3(a):
    high = a.astype(bf16)
    rest = a - high.astype(f32)
    mid = rest.astype(bf16)
    return high, mid, (rest - mid.astype(f32)).astype(bf16)


def mul(a, b, dims):
    return lax.dot_general(a, b, (dims, ((), ())), preferred_element_type=f32)


def mul3(a, b, dims):
    (ah, al), (bh, bl) = a, b
    return mul(ah, bh, dims) + (mul(ah, bl, dims) + mul(al, bh, dims))


NN = ((1,), (0,))
NT = ((1,), (1,))
TN = ((0,), (0,))


def pick_kernel(
    width, place_ref, pivots_hbm, emb_hbm, fac_hbm, out_ref, pivots_ref, emb_ref, fac_ref, sems
):
    copies = [
        pltpu.make_async_copy(src, dst, sems.at[i])
        for i, (src, dst) in enumerate(
            ((pivots_hbm, pivots_ref), (emb_hbm, emb_ref), (fac_hbm, fac_ref))
        )
    ]
    for copy in copies:
        copy.start()
    copies[0].wait()
    base, core = place_ref[0], place_ref[1]
    rows_dev = emb_ref.shape[0]
    count = pivots_ref.shape[1]
    local = (pivots_ref[...] - base).astype(f32)
    order = lax.broadcasted_iota(jnp.int32, (1, count), 1).astype(f32)
    inside = jnp.where((local >= 0) & (local < rows_dev), 1.0, 0.0)
    sub = lax.broadcasted_iota(jnp.int32, (8, rows_dev), 0)
    lane = lax.broadcasted_iota(jnp.int32, (8, rows_dev), 1).astype(f32)
    sub_tag = lax.broadcasted_iota(jnp.int32, (8, BLOCK), 0)
    hot = jnp.zeros((8, rows_dev), f32)
    tag = jnp.full((8, BLOCK), -1.0, f32)
    for k in range(SLOTS):
        pos = jnp.min(jnp.where(inside > 0, order, float(count)), axis=1, keepdims=True)
        hit = order == pos
        row = jnp.sum(jnp.where(hit, local, 0.0), axis=1, keepdims=True)
        valid = pos < count
        row = jnp.where(valid, row, -1.0)
        hot = hot + jnp.where((sub == k) & (lane == row), 1.0, 0.0)
        tag = jnp.where((sub_tag == k), jnp.where(valid, pos, -1.0), tag)
        inside = jnp.where(hit, 0.0, inside)
    hot = hot.astype(bf16)
    pieces = []
    for ref, copy in ((emb_ref, copies[1]), (fac_ref, copies[2])):
        copy.wait()
        for c in range(0, ref.shape[1], 256):
            high, mid, low = split3(ref[:, c : c + 256])
            pieces.append(mul(hot, high, NN) + (mul(hot, mid, NN) + mul(hot, low, NN)))
    rows = jnp.concatenate(pieces + [jnp.zeros((8, BLOCK), f32)], axis=1)
    lane_out = lax.broadcasted_iota(jnp.int32, (8, BLOCK), 1)
    for j in range(out_ref.shape[0]):
        first = width * j
        tile = first // BLOCK * BLOCK
        window = rows[:, tile : tile + 2 * BLOCK]
        if first > tile:
            window = pltpu.roll(window, 2 * BLOCK - (first - tile), 1)
        piece = jnp.where(lane_out < width, window[:, :BLOCK], jnp.where(lane_out == width, tag, 0.0))
        piece = jnp.where(core == 0, piece, pltpu.roll(piece, BLOCK // 2, 1))
        out_ref[j] = piece


def select_kernel(width, slots_ref, out_ref):
    slots = slots_ref[...]
    count = out_ref.shape[1]
    order = lax.broadcasted_iota(jnp.int32, (1, count), 1).astype(f32)
    half = BLOCK // 2
    parts = split3(slots)
    total = None
    for c in range(2):
        tag = slots[:, c * half + width : c * half + width + 1]
        hot = jnp.where(tag == order, 1.0, 0.0).astype(bf16)
        for part in parts:
            got = mul(part, hot, TN)[c * half : c * half + width]
            total = got if total is None else total + got
    out_ref[...] = total


def factor_block(mat_ref, off, inv_ref, d_ref, e_ref):
    d_ref[...] = mat_ref[pl.ds(off, BLOCK), pl.ds(off, BLOCK)]
    e_ref[...] = jnp.where(
        lax.broadcasted_iota(jnp.int32, (BLOCK, BLOCK), 0)
        == lax.broadcasted_iota(jnp.int32, (BLOCK, BLOCK), 1),
        1.0,
        0.0,
    ).astype(f32)
    full = (PANEL, BLOCK)

    def spread(a, lane):
        return jnp.broadcast_to(a[:, lane : lane + 1], full)

    for p in range(BLOCK // PANEL):
        first = p * PANEL
        rows = [jnp.broadcast_to(d_ref[first + k : first + k + 1, :], full) for k in range(PANEL)]
        invs = [jnp.broadcast_to(e_ref[first + k : first + k + 1, :], full) for k in range(PANEL)]
        s = [[spread(rows[i], first + k) for k in range(i + 1)] for i in range(PANEL)]
        scale = []
        for k in range(PANEL):
            r = lax.rsqrt(s[k][k])
            scale.append(r)
            for i in range(k + 1, PANEL):
                s[i][k] = s[i][k] * r
            for i in range(k + 1, PANEL):
                for j in range(k + 1, i + 1):
                    s[i][j] = s[i][j] - s[i][k] * s[j][k]
        for k in range(PANEL):
            for m in range(k):
                rows[k] = rows[k] - s[k][m] * rows[m]
                invs[k] = invs[k] - s[k][m] * invs[m]
            rows[k] = rows[k] * scale[k]
            invs[k] = invs[k] * scale[k]
            inv_ref[first + k : first + k + 1, :] = invs[k][0:1, :]
        for b in range(p + 1, BLOCK // PANEL):
            at = slice(b * PANEL, (b + 1) * PANEL)
            d = d_ref[at, :]
            e = e_ref[at, :]
            cols = [spread(d, first + k) for k in range(PANEL)]
            for k in range(PANEL):
                for m in range(k):
                    cols[k] = cols[k] - s[k][m] * cols[m]
                cols[k] = cols[k] * scale[k]
            for k in range(PANEL):
                d = d - cols[k] * rows[k]
                e = e - cols[k] * invs[k]
            d_ref[at, :] = d
            e_ref[at, :] = e


def main_kernel(
    place_ref, emb_ref, fac_ref, own_ref, other_ref, new_ref, keep_ref, send_ref,
    ch_ref, cl_ref, sq_ref, mat_ref, inv_ref, d_ref, e_ref, sum_ref,
):
    core = place_ref[1]
    rows_dev, width = emb_ref.shape
    old_rank = fac_ref.shape[1]
    half, count = own_ref.shape
    total = 2 * half
    second = width - half
    scale = 1.0 / (2.0 * width)

    def take(ref, which):
        start = pl.multiple_of(which * half, BLOCK)
        sq = jnp.zeros((1, count), f32)
        for r in range(0, half, BLOCK):
            a = ref[r : r + BLOCK, :]
            high, low = split2(a)
            at = pl.ds(pl.multiple_of(start + r, BLOCK), BLOCK)
            ch_ref[at, :] = high
            cl_ref[at, :] = low
            part = jnp.sum(a * a, axis=0, keepdims=True)
            if r >= second:
                part = jnp.where(which == 0, part, 0.0)
            sq = sq + part
        return sq

    sq = take(own_ref, core) + take(other_ref, 1 - core)
    sq_ref[...] = jnp.transpose(jnp.broadcast_to(sq, (BLOCK, count)))

    def wide(lo, hi, need):
        return ch_ref[lo:hi, :need], cl_ref[lo:hi, :need]

    for i in range(count // BLOCK):
        at = slice(i * BLOCK, (i + 1) * BLOCK)
        need = (i // 2 + 1) * 2 * BLOCK
        cross = mul3((ch_ref[:width, at], cl_ref[:width, at]), wide(0, width, need), TN)
        old = mul3((ch_ref[width:, at], cl_ref[width:, at]), wide(width, total, need), TN)
        left = sq_ref[at, 0:1]
        block = jnp.exp((2.0 * cross - (left + sq[:, :need])) * scale) - old
        row = lax.broadcasted_iota(jnp.int32, (BLOCK, need), 0) + i * BLOCK
        col = lax.broadcasted_iota(jnp.int32, (BLOCK, need), 1)
        mat_ref[at, :need] = block + jnp.where(row == col, ridge_term, 0.0)
    for i in range(rows_dev // BLOCK):
        at = slice(i * BLOCK, (i + 1) * BLOCK)
        a = emb_ref[at, :]
        cross = mul3(split2(a), wide(0, width, count), NN)
        old = mul3(split2(fac_ref[at, :]), wide(width, total, count), NN)
        left = jnp.sum(a * a, axis=1, keepdims=True)
        mat_ref[count + i * BLOCK : count + (i + 1) * BLOCK, :] = (
            jnp.exp((2.0 * cross - (left + sq)) * scale) - old
        )

    all_rows = count + rows_dev

    def step(kb, carry):
        off = pl.multiple_of(kb * BLOCK, BLOCK)
        factor_block(mat_ref, off, inv_ref, d_ref, e_ref)
        panel = mul3(split2(mat_ref[:, pl.ds(off, BLOCK)]), split2(inv_ref[...]), NT)
        new_ref[:, pl.ds(off, BLOCK)] = panel[count:]
        row = lax.broadcasted_iota(jnp.int32, (all_rows, BLOCK), 0)
        panel = jnp.where(row >= off + BLOCK, panel, 0.0)
        high, low = split2(panel)
        for r in range(0, all_rows, 256):
            for c in range(0, min(r + 256, count), 256):

                @pl.when(off + BLOCK < min(r, c) + 256)
                def _():
                    mat_ref[r : r + 256, c : c + 256] = mat_ref[r : r + 256, c : c + 256] - mul3(
                        (high[r : r + 256], low[r : r + 256]), (high[c : c + 256], low[c : c + 256]), NT
                    )

        return carry

    lax.fori_loop(0, count // BLOCK, step, 0)

    new = split2(new_ref[...])
    for i in range(old_rank // BLOCK):
        at = slice(i * BLOCK, (i + 1) * BLOCK)
        sum_ref[at, :] = mul3(split2(fac_ref[:, at]), new, TN)
    for i in range(count // BLOCK):
        at = slice(i * BLOCK, (i + 1) * BLOCK)
        sum_ref[old_rank + i * BLOCK : old_rank + (i + 1) * BLOCK, :] = mul3(
            (new[0][:, at], new[1][:, at]), new, TN
        )
    _, n_zh, part, _ = keep_ref.shape
    shares = keep_ref.shape[0]
    for zh in range(n_zh):
        for j in range(shares):
            start = (zh * shares + j) * 2 * part
            keep_ref[j, zh] = sum_ref[pl.ds(pl.multiple_of(start + core * part, part), part), :]
            send_ref[j, zh] = sum_ref[pl.ds(pl.multiple_of(start + (1 - core) * part, part), part), :]


VMEM = pl.BlockSpec(memory_space=pltpu.VMEM)
SMEM = pl.BlockSpec(memory_space=pltpu.SMEM)
HBM = pl.BlockSpec(memory_space=pltpu.HBM)
PARAMS = pltpu.CompilerParams(vmem_limit_bytes=24 * 1024 * 1024)
WIDE_PARAMS = pltpu.CompilerParams(vmem_limit_bytes=60 * 1024 * 1024)


def on_device(n_xy, n_z, embeddings, factor, pivots):
    rows_dev, width = embeddings.shape
    old_rank = factor.shape[1]
    count = pivots.shape[0]
    total = width + old_rank
    slices = 2 * n_xy
    piece = total // slices
    core = lax.axis_index("core")
    mine = lax.axis_index(("zl", "core", "zh", "x", "y"))
    place = jnp.stack([mine * rows_dev, core]).astype(jnp.int32)
    sent = pl.pallas_call(
        functools.partial(pick_kernel, piece),
        out_shape=jax.ShapeDtypeStruct((slices, 8, BLOCK), f32),
        in_specs=[SMEM, HBM, HBM, HBM],
        out_specs=VMEM,
        scratch_shapes=[
            pltpu.VMEM((1, count), jnp.int32),
            pltpu.VMEM((rows_dev, width), f32),
            pltpu.VMEM((rows_dev, old_rank), f32),
            pltpu.SemaphoreType.DMA((3,)),
        ],
        compiler_params=WIDE_PARAMS,
        name="pick",
    )(place, pivots.reshape(1, count), embeddings, factor)
    got = lax.all_to_all(sent, ("core", "x", "y"), 0, 0, tiled=True)
    packed = (got[:n_xy] + got[n_xy:])[:, :SLOTS].reshape(n_xy * SLOTS, BLOCK)
    packed = jnp.broadcast_to(packed[None], (n_z, n_xy * SLOTS, BLOCK))
    slots = lax.all_to_all(packed, ("zl", "zh"), 0, 0, tiled=True)
    chosen_slice = pl.pallas_call(
        functools.partial(select_kernel, piece),
        out_shape=jax.ShapeDtypeStruct((piece, count), f32),
        in_specs=[VMEM],
        out_specs=VMEM,
        compiler_params=PARAMS,
        name="select",
    )(slots.reshape(n_z * n_xy * SLOTS, BLOCK))
    wide = jnp.broadcast_to(chosen_slice[None], (n_xy, piece, count))
    own = lax.all_to_all(wide, ("x", "y"), 0, 0, tiled=True).reshape(n_xy * piece, count)
    other = lax.ppermute(own, "core", [(0, 1), (1, 0)])
    share = (old_rank + count) // slices
    part = share // 2
    split = jax.ShapeDtypeStruct((n_xy, 2, part, count), f32)
    new_factor, keep, send = pl.pallas_call(
        main_kernel,
        out_shape=(jax.ShapeDtypeStruct((rows_dev, count), f32), split, split),
        in_specs=[SMEM, VMEM, VMEM, VMEM, VMEM],
        out_specs=(VMEM, VMEM, VMEM),
        scratch_shapes=[
            pltpu.VMEM((total, count), bf16),
            pltpu.VMEM((total, count), bf16),
            pltpu.VMEM((count, BLOCK), f32),
            pltpu.VMEM((count + rows_dev, count), f32),
            pltpu.VMEM((BLOCK, BLOCK), f32),
            pltpu.VMEM((BLOCK, BLOCK), f32),
            pltpu.VMEM((BLOCK, BLOCK), f32),
            pltpu.VMEM((old_rank + count, count), f32),
        ],
        compiler_params=PARAMS,
        name="main",
    )(place, embeddings, factor, own, other)
    pair = keep + lax.ppermute(send, "core", [(0, 1), (1, 0)])
    layer = jnp.sum(lax.all_to_all(pair, ("x", "y"), 0, 0, tiled=True), axis=0)
    n_zl = n_z // 2
    few = part // n_zl
    spread = jnp.swapaxes(layer.reshape(2, n_zl, few, count), 0, 1).reshape(n_z, few, count)
    summed = jnp.sum(lax.all_to_all(spread, ("zl", "zh"), 0, 0, tiled=True), axis=0)
    my_dev = lax.axis_index(("zh", "x", "y"))
    first = my_dev * share + core * part + lax.axis_index("zl") * few
    diagonal_hit = first + jnp.arange(few)[:, None] - old_rank == jnp.arange(count)[None, :]
    summed = summed + core_ridge * diagonal_hit.astype(f32)
    line = jnp.broadcast_to(summed[None], (n_zl, few, count))
    line = lax.all_to_all(line, "zl", 0, 0, tiled=True).reshape(part, count)
    return new_factor, lax.all_gather(line, "core", axis=0, tiled=True)


def solution(mesh):
    n_zl, n_zh, n_x = 8, 2, 4
    n_y = mesh.shape["dev"] // (n_zh * n_x)
    n_core = mesh.shape["grp"] // n_zl
    axes = ("zl", "core", "zh", "x", "y")
    fine = Mesh(mesh.devices.reshape(n_zl, n_core, n_zh, n_x, n_y), axes)
    in_specs = (P(axes, None), P(axes, None), P())
    out_specs = (P(axes, None), P(("zh", "x", "y"), None))
    return jax.shard_map(
        functools.partial(on_device, n_x * n_y, n_zl * n_zh),
        mesh=fine, in_specs=in_specs, out_specs=out_specs, check_vma=False,
    )
```

```python
import functools

import jax
import jax.numpy as jnp
from jax import lax
from jax.experimental import pallas as pl
from jax.experimental.pallas import tpu as pltpu
from jax.sharding import Mesh
from jax.sharding import PartitionSpec as P

ridge_term = 1.0
core_ridge = 1.0

SLOTS = 3
BLOCK = 128
PANEL = 8
f32 = jnp.float32
bf16 = jnp.bfloat16


def split2(a):
    high = a.astype(bf16)
    return high, (a - high.astype(f32)).astype(bf16)


def split3(a):
    high = a.astype(bf16)
    rest = a - high.astype(f32)
    mid = rest.astype(bf16)
    return high, mid, (rest - mid.astype(f32)).astype(bf16)


def mul(a, b, dims):
    return lax.dot_general(a, b, (dims, ((), ())), preferred_element_type=f32)


def mul3(a, b, dims):
    (ah, al), (bh, bl) = a, b
    return mul(ah, bh, dims) + (mul(ah, bl, dims) + mul(al, bh, dims))


NN = ((1,), (0,))
NT = ((1,), (1,))
TN = ((0,), (0,))


def pick_kernel(
    width, base_ref, core_ref, pivots_hbm, emb_hbm, fac_hbm, out_ref, pivots_ref, emb_ref, fac_ref, sems
):
    copies = [
        pltpu.make_async_copy(src, dst, sems.at[i])
        for i, (src, dst) in enumerate(
            ((pivots_hbm, pivots_ref), (emb_hbm, emb_ref), (fac_hbm, fac_ref))
        )
    ]
    for copy in copies:
        copy.start()
    copies[0].wait()
    base, core = base_ref[0], core_ref[0]
    rows_dev = emb_ref.shape[0]
    count = pivots_ref.shape[1]
    local = (pivots_ref[...] - base).astype(f32)
    order = lax.broadcasted_iota(jnp.int32, (1, count), 1).astype(f32)
    inside = jnp.where((local >= 0) & (local < rows_dev), 1.0, 0.0)
    sub = lax.broadcasted_iota(jnp.int32, (8, rows_dev), 0)
    lane = lax.broadcasted_iota(jnp.int32, (8, rows_dev), 1).astype(f32)
    sub_tag = lax.broadcasted_iota(jnp.int32, (8, BLOCK), 0)
    hot = jnp.zeros((8, rows_dev), f32)
    tag = jnp.full((8, BLOCK), -1.0, f32)
    for k in range(SLOTS):
        pos = jnp.min(jnp.where(inside > 0, order, float(count)), axis=1, keepdims=True)
        hit = order == pos
        row = jnp.sum(jnp.where(hit, local, 0.0), axis=1, keepdims=True)
        valid = pos < count
        row = jnp.where(valid, row, -1.0)
        hot = hot + jnp.where((sub == k) & (lane == row), 1.0, 0.0)
        tag = jnp.where((sub_tag == k), jnp.where(valid, pos, -1.0), tag)
        inside = jnp.where(hit, 0.0, inside)
    hot = hot.astype(bf16)
    copies[1].wait()
    copies[2].wait()
    pieces = []
    for h in range(2):
        for ref in (emb_ref, fac_ref):
            step = ref.shape[1] // 2
            high, mid, low = split3(ref[:, h * step : (h + 1) * step])
            pieces.append(mul(hot, high, NN) + (mul(hot, mid, NN) + mul(hot, low, NN)))
    rows = jnp.concatenate(pieces + [jnp.zeros((8, BLOCK), f32)], axis=1)
    lane_out = lax.broadcasted_iota(jnp.int32, (8, BLOCK), 1)
    for j in range(out_ref.shape[0]):
        first = width * j
        tile = first // BLOCK * BLOCK
        window = rows[:, tile : tile + 2 * BLOCK]
        if first > tile:
            window = pltpu.roll(window, 2 * BLOCK - (first - tile), 1)
        piece = jnp.where(lane_out < width, window[:, :BLOCK], jnp.where(lane_out == width, tag, 0.0))
        piece = jnp.where(core == 0, piece, pltpu.roll(piece, BLOCK // 2, 1))
        out_ref[j] = piece


def select_kernel(width, slots_ref, out_ref):
    slots = slots_ref[...]
    count = out_ref.shape[1]
    order = lax.broadcasted_iota(jnp.int32, (1, count), 1).astype(f32)
    half = BLOCK // 2
    parts = split3(slots)
    total = None
    for c in range(2):
        tag = slots[:, c * half + width : c * half + width + 1]
        hot = jnp.where(tag == order, 1.0, 0.0).astype(bf16)
        for part in parts:
            got = mul(part, hot, TN)[c * half : c * half + width]
            total = got if total is None else total + got
    out_ref[...] = total


def factor_block(mat_ref, off, inv_ref, d_ref, e_ref):
    d_ref[...] = mat_ref[pl.ds(off, BLOCK), pl.ds(off, BLOCK)]
    e_ref[...] = jnp.where(
        lax.broadcasted_iota(jnp.int32, (BLOCK, BLOCK), 0)
        == lax.broadcasted_iota(jnp.int32, (BLOCK, BLOCK), 1),
        1.0,
        0.0,
    ).astype(f32)
    full = (PANEL, BLOCK)

    def spread(a, lane):
        return jnp.broadcast_to(a[:, lane : lane + 1], full)

    for p in range(BLOCK // PANEL):
        first = p * PANEL
        rows = [jnp.broadcast_to(d_ref[first + k : first + k + 1, :], full) for k in range(PANEL)]
        invs = [jnp.broadcast_to(e_ref[first + k : first + k + 1, :], full) for k in range(PANEL)]
        s = [[spread(rows[i], first + k) for k in range(i + 1)] for i in range(PANEL)]
        scale = []
        for k in range(PANEL):
            r = lax.rsqrt(s[k][k])
            scale.append(r)
            for i in range(k + 1, PANEL):
                s[i][k] = s[i][k] * r
            for i in range(k + 1, PANEL):
                for j in range(k + 1, i + 1):
                    s[i][j] = s[i][j] - s[i][k] * s[j][k]
        for k in range(PANEL):
            for m in range(k):
                rows[k] = rows[k] - s[k][m] * rows[m]
                invs[k] = invs[k] - s[k][m] * invs[m]
            rows[k] = rows[k] * scale[k]
            invs[k] = invs[k] * scale[k]
            inv_ref[first + k : first + k + 1, :] = invs[k][0:1, :]
        for b in range(p + 1, BLOCK // PANEL):
            at = slice(b * PANEL, (b + 1) * PANEL)
            d = d_ref[at, :]
            e = e_ref[at, :]
            cols = [spread(d, first + k) for k in range(PANEL)]
            for k in range(PANEL):
                for m in range(k):
                    cols[k] = cols[k] - s[k][m] * cols[m]
                cols[k] = cols[k] * scale[k]
            for k in range(PANEL):
                d = d - cols[k] * rows[k]
                e = e - cols[k] * invs[k]
            d_ref[at, :] = d
            e_ref[at, :] = e


def load_half(src_ref, emb_part, ch_ref, cl_ref):
    half, count = src_ref.shape
    sq = jnp.zeros((1, count), f32)
    for r in range(0, half, BLOCK):
        a = src_ref[r : r + BLOCK, :]
        ch_ref[r : r + BLOCK, :], cl_ref[r : r + BLOCK, :] = split2(a)
        if r < emb_part:
            sq = sq + jnp.sum(a * a, axis=0, keepdims=True)
    return sq


def products(which, emb_ref, fac_ref, ch_ref, cl_ref, emit):
    half, count = ch_ref.shape
    emb_part, fac_part = emb_ref.shape[1] // 2, fac_ref.shape[1] // 2

    def wide(lo, hi, need):
        return ch_ref[lo:hi, :need], cl_ref[lo:hi, :need]

    for i in range(count // BLOCK):
        at = slice(i * BLOCK, (i + 1) * BLOCK)
        need = (i // 2 + 1) * 2 * BLOCK
        cross = mul3((ch_ref[:emb_part, at], cl_ref[:emb_part, at]), wide(0, emb_part, need), TN)
        old = mul3((ch_ref[emb_part:, at], cl_ref[emb_part:, at]), wide(emb_part, half, need), TN)
        emit(i * BLOCK, need, cross, old)
    emb_at = pl.ds(pl.multiple_of(which * emb_part, BLOCK), emb_part)
    fac_at = pl.ds(pl.multiple_of(which * fac_part, BLOCK), fac_part)
    for r in range(0, emb_ref.shape[0], BLOCK):
        cross = mul3(split2(emb_ref[r : r + BLOCK, emb_at]), wide(0, emb_part, count), NN)
        old = mul3(split2(fac_ref[r : r + BLOCK, fac_at]), wide(emb_part, half, count), NN)
        emit(count + r, count, cross, old)


def first_kernel(core_ref, emb_ref, fac_ref, own_ref, cross_ref, old_ref, sq_ref, ch_ref, cl_ref):
    sq = load_half(own_ref, emb_ref.shape[1] // 2, ch_ref, cl_ref)
    sq_ref[...] = jnp.broadcast_to(sq, sq_ref.shape)

    def emit(row, need, cross, old):
        cross_ref[row : row + BLOCK, :need] = cross
        old_ref[row : row + BLOCK, :need] = old

    products(core_ref[0], emb_ref, fac_ref, ch_ref, cl_ref, emit)


def main_kernel(
    core_ref, emb_ref, fac_ref, other_ref, cross_ref, old_ref, own_sq_ref,
    new_ref, keep_ref, send_ref,
    ch_ref, cl_ref, sq_ref, mat_ref, inv_ref, d_ref, e_ref, sum_ref,
):
    core = core_ref[0]
    rows_dev, width = emb_ref.shape
    old_rank = fac_ref.shape[1]
    count = other_ref.shape[1]
    scale = 1.0 / (2.0 * width)
    sq = own_sq_ref[0:1, :] + load_half(other_ref, width // 2, ch_ref, cl_ref)
    sq_ref[...] = jnp.transpose(jnp.broadcast_to(sq, (BLOCK, count)))

    def emit(row, need, cross, old):
        at = slice(row, row + BLOCK)
        cross = cross_ref[at, :need] + cross
        old = old_ref[at, :need] + old
        if row < count:
            left = sq_ref[at, 0:1]
        else:
            a = emb_ref[row - count : row - count + BLOCK, :]
            left = jnp.sum(a * a, axis=1, keepdims=True)
        block = jnp.exp((2.0 * cross - (left + sq[:, :need])) * scale) - old
        if row < count:
            r = lax.broadcasted_iota(jnp.int32, (BLOCK, need), 0) + row
            c = lax.broadcasted_iota(jnp.int32, (BLOCK, need), 1)
            block = block + jnp.where(r == c, ridge_term, 0.0)
        mat_ref[at, :need] = block

    products(1 - core, emb_ref, fac_ref, ch_ref, cl_ref, emit)

    all_rows = count + rows_dev

    def step(kb, carry):
        off = pl.multiple_of(kb * BLOCK, BLOCK)
        factor_block(mat_ref, off, inv_ref, d_ref, e_ref)
        panel = mul3(split2(mat_ref[:, pl.ds(off, BLOCK)]), split2(inv_ref[...]), NT)
        new_ref[:, pl.ds(off, BLOCK)] = panel[count:]
        row = lax.broadcasted_iota(jnp.int32, (all_rows, BLOCK), 0)
        panel = jnp.where(row >= off + BLOCK, panel, 0.0)
        high, low = split2(panel)
        for r in range(0, all_rows, 256):
            for c in range(0, min(r + 256, count), 256):

                @pl.when(off + BLOCK < min(r, c) + 256)
                def _():
                    mat_ref[r : r + 256, c : c + 256] = mat_ref[r : r + 256, c : c + 256] - mul3(
                        (high[r : r + 256], low[r : r + 256]), (high[c : c + 256], low[c : c + 256]), NT
                    )

        return carry

    lax.fori_loop(0, count // BLOCK, step, 0)

    new = split2(new_ref[...])
    for i in range(old_rank // BLOCK):
        at = slice(i * BLOCK, (i + 1) * BLOCK)
        sum_ref[at, :] = mul3(split2(fac_ref[:, at]), new, TN)
    for i in range(count // BLOCK):
        at = slice(i * BLOCK, (i + 1) * BLOCK)
        sum_ref[old_rank + i * BLOCK : old_rank + (i + 1) * BLOCK, :] = mul3(
            (new[0][:, at], new[1][:, at]), new, TN
        )
    _, n_zh, part, _ = keep_ref.shape
    shares = keep_ref.shape[0]
    for zh in range(n_zh):
        for j in range(shares):
            start = (zh * shares + j) * 2 * part
            keep_ref[j, zh] = sum_ref[pl.ds(pl.multiple_of(start + core * part, part), part), :]
            send_ref[j, zh] = sum_ref[pl.ds(pl.multiple_of(start + (1 - core) * part, part), part), :]


VMEM = pl.BlockSpec(memory_space=pltpu.VMEM)
SMEM = pl.BlockSpec(memory_space=pltpu.SMEM)
HBM = pl.BlockSpec(memory_space=pltpu.HBM)
PARAMS = pltpu.CompilerParams(vmem_limit_bytes=24 * 1024 * 1024)
WIDE_PARAMS = pltpu.CompilerParams(vmem_limit_bytes=60 * 1024 * 1024)


def on_device(n_xy, n_z, embeddings, factor, pivots):
    rows_dev, width = embeddings.shape
    old_rank = factor.shape[1]
    count = pivots.shape[0]
    total = width + old_rank
    slices = 2 * n_xy
    piece = total // slices
    core = lax.axis_index("core")
    mine = lax.axis_index(("zl", "core", "zh", "x", "y"))
    base_place = (mine * rows_dev).astype(jnp.int32).reshape(1)
    core_place = core.astype(jnp.int32).reshape(1)
    sent = pl.pallas_call(
        functools.partial(pick_kernel, piece),
        out_shape=jax.ShapeDtypeStruct((slices, 8, BLOCK), f32),
        in_specs=[SMEM, SMEM, HBM, HBM, HBM],
        out_specs=VMEM,
        scratch_shapes=[
            pltpu.VMEM((1, count), jnp.int32),
            pltpu.VMEM((rows_dev, width), f32),
            pltpu.VMEM((rows_dev, old_rank), f32),
            pltpu.SemaphoreType.DMA((3,)),
        ],
        compiler_params=WIDE_PARAMS,
        name="pick",
    )(base_place, core_place, pivots.reshape(1, count), embeddings, factor)
    got = lax.all_to_all(sent, ("core", "x", "y"), 0, 0, tiled=True)
    packed = (got[:n_xy] + got[n_xy:])[:, :SLOTS].reshape(n_xy * SLOTS, BLOCK)
    packed = jnp.broadcast_to(packed[None], (n_z, n_xy * SLOTS, BLOCK))
    slots = lax.all_to_all(packed, ("zl", "zh"), 0, 0, tiled=True)
    chosen_slice = pl.pallas_call(
        functools.partial(select_kernel, piece),
        out_shape=jax.ShapeDtypeStruct((piece, count), f32),
        in_specs=[VMEM],
        out_specs=VMEM,
        compiler_params=PARAMS,
        name="select",
    )(slots.reshape(n_z * n_xy * SLOTS, BLOCK))
    wide = jnp.broadcast_to(chosen_slice[None], (n_xy, piece, count))
    own = lax.all_to_all(wide, ("x", "y"), 0, 0, tiled=True).reshape(n_xy * piece, count)
    other = lax.ppermute(own, "core", [(0, 1), (1, 0)])
    half = total // 2
    all_rows = count + rows_dev
    halves = [pltpu.VMEM((half, count), bf16), pltpu.VMEM((half, count), bf16)]
    table = jax.ShapeDtypeStruct((all_rows, count), f32)
    cross, old, own_sq = pl.pallas_call(
        first_kernel,
        out_shape=(table, table, jax.ShapeDtypeStruct((8, count), f32)),
        in_specs=[SMEM, VMEM, VMEM, VMEM],
        out_specs=(VMEM, VMEM, VMEM),
        scratch_shapes=halves,
        compiler_params=PARAMS,
        cost_estimate=pl.CostEstimate(
            flops=6 * half * count * all_rows, bytes_accessed=4 * half * count, transcendentals=0
        ),
        name="first",
    )(core_place, embeddings, factor, own)
    share = (old_rank + count) // slices
    part = share // 2
    split = jax.ShapeDtypeStruct((n_xy, 2, part, count), f32)
    new_factor, keep, send = pl.pallas_call(
        main_kernel,
        out_shape=(jax.ShapeDtypeStruct((rows_dev, count), f32), split, split),
        in_specs=[SMEM] + [VMEM] * 6,
        out_specs=(VMEM, VMEM, VMEM),
        scratch_shapes=halves + [
            pltpu.VMEM((count, BLOCK), f32),
            pltpu.VMEM((count + rows_dev, count), f32),
            pltpu.VMEM((BLOCK, BLOCK), f32),
            pltpu.VMEM((BLOCK, BLOCK), f32),
            pltpu.VMEM((BLOCK, BLOCK), f32),
            pltpu.VMEM((old_rank + count, count), f32),
        ],
        compiler_params=PARAMS,
        name="main",
    )(core_place, embeddings, factor, other, cross, old, own_sq)
    pair = keep + lax.ppermute(send, "core", [(0, 1), (1, 0)])
    layer = jnp.sum(lax.all_to_all(pair, ("x", "y"), 0, 0, tiled=True), axis=0)
    n_zl = n_z // 2
    few = part // n_zl
    spread = jnp.swapaxes(layer.reshape(2, n_zl, few, count), 0, 1).reshape(n_z, few, count)
    summed = jnp.sum(lax.all_to_all(spread, ("zl", "zh"), 0, 0, tiled=True), axis=0)
    my_dev = lax.axis_index(("zh", "x", "y"))
    first = my_dev * share + core * part + lax.axis_index("zl") * few
    diagonal_hit = first + jnp.arange(few)[:, None] - old_rank == jnp.arange(count)[None, :]
    summed = summed + core_ridge * diagonal_hit.astype(f32)
    line = jnp.broadcast_to(summed[None], (n_zl, few, count))
    line = lax.all_to_all(line, "zl", 0, 0, tiled=True).reshape(part, count)
    return new_factor, lax.all_gather(line, "core", axis=0, tiled=True)


def solution(mesh):
    n_zl, n_zh, n_x = 8, 2, 4
    n_y = mesh.shape["dev"] // (n_zh * n_x)
    n_core = mesh.shape["grp"] // n_zl
    axes = ("zl", "core", "zh", "x", "y")
    fine = Mesh(mesh.devices.reshape(n_zl, n_core, n_zh, n_x, n_y), axes)
    in_specs = (P(axes, None), P(axes, None), P())
    out_specs = (P(axes, None), P(("zh", "x", "y"), None))
    return jax.shard_map(
        functools.partial(on_device, n_x * n_y, n_zl * n_zh),
        mesh=fine, in_specs=in_specs, out_specs=out_specs, check_vma=False,
    )
```

```python
import functools

import jax
import jax.numpy as jnp
from jax import lax
from jax.experimental import pallas as pl
from jax.experimental.pallas import tpu as pltpu
from jax.sharding import Mesh
from jax.sharding import PartitionSpec as P

ridge_term = 1.0
core_ridge = 1.0

SLOTS = 3
BLOCK = 128
PANEL = 8
f32 = jnp.float32
bf16 = jnp.bfloat16


def split2(a):
    high = a.astype(bf16)
    return high, (a - high.astype(f32)).astype(bf16)


def split3(a):
    high = a.astype(bf16)
    rest = a - high.astype(f32)
    mid = rest.astype(bf16)
    return high, mid, (rest - mid.astype(f32)).astype(bf16)


def mul(a, b, dims):
    return lax.dot_general(a, b, (dims, ((), ())), preferred_element_type=f32)


def mul3(a, b, dims):
    (ah, al), (bh, bl) = a, b
    return mul(ah, bh, dims) + (mul(ah, bl, dims) + mul(al, bh, dims))


NN = ((1,), (0,))
NT = ((1,), (1,))
TN = ((0,), (0,))


def pick_kernel(
    width, base_ref, core_ref, pivots_hbm, emb_hbm, fac_hbm, out_ref, pivots_ref, emb_ref, fac_ref, sems
):
    copies = [
        pltpu.make_async_copy(src, dst, sems.at[i])
        for i, (src, dst) in enumerate(
            ((pivots_hbm, pivots_ref), (emb_hbm, emb_ref), (fac_hbm, fac_ref))
        )
    ]
    for copy in copies:
        copy.start()
    copies[0].wait()
    base, core = base_ref[0], core_ref[0]
    rows_dev = emb_ref.shape[0]
    count = pivots_ref.shape[1]
    local = (pivots_ref[...] - base).astype(f32)
    order = lax.broadcasted_iota(jnp.int32, (1, count), 1).astype(f32)
    inside = jnp.where((local >= 0) & (local < rows_dev), 1.0, 0.0)
    sub = lax.broadcasted_iota(jnp.int32, (8, rows_dev), 0)
    lane = lax.broadcasted_iota(jnp.int32, (8, rows_dev), 1).astype(f32)
    sub_tag = lax.broadcasted_iota(jnp.int32, (8, BLOCK), 0)
    hot = jnp.zeros((8, rows_dev), f32)
    tag = jnp.full((8, BLOCK), -1.0, f32)
    for k in range(SLOTS):
        pos = jnp.min(jnp.where(inside > 0, order, float(count)), axis=1, keepdims=True)
        hit = order == pos
        row = jnp.sum(jnp.where(hit, local, 0.0), axis=1, keepdims=True)
        valid = pos < count
        row = jnp.where(valid, row, -1.0)
        hot = hot + jnp.where((sub == k) & (lane == row), 1.0, 0.0)
        tag = jnp.where((sub_tag == k), jnp.where(valid, pos, -1.0), tag)
        inside = jnp.where(hit, 0.0, inside)
    hot = hot.astype(bf16)
    copies[1].wait()
    copies[2].wait()
    pieces = []
    for h in range(2):
        for ref in (emb_ref, fac_ref):
            step = ref.shape[1] // 2
            high, mid, low = split3(ref[:, h * step : (h + 1) * step])
            pieces.append(mul(hot, high, NN) + (mul(hot, mid, NN) + mul(hot, low, NN)))
    rows = jnp.concatenate(pieces + [jnp.zeros((8, BLOCK), f32)], axis=1)
    lane_out = lax.broadcasted_iota(jnp.int32, (8, BLOCK), 1)
    for j in range(out_ref.shape[0]):
        first = width * j
        tile = first // BLOCK * BLOCK
        window = rows[:, tile : tile + 2 * BLOCK]
        if first > tile:
            window = pltpu.roll(window, 2 * BLOCK - (first - tile), 1)
        piece = jnp.where(lane_out < width, window[:, :BLOCK], jnp.where(lane_out == width, tag, 0.0))
        piece = jnp.where(core == 0, piece, pltpu.roll(piece, BLOCK // 2, 1))
        out_ref[j] = piece[:4]


def select_kernel(width, slots_ref, out_ref):
    slots = slots_ref[...]
    count = out_ref.shape[1]
    order = lax.broadcasted_iota(jnp.int32, (1, count), 1).astype(f32)
    half = BLOCK // 2
    parts = split3(slots)
    total = None
    for c in range(2):
        tag = slots[:, c * half + width : c * half + width + 1]
        hot = jnp.where(tag == order, 1.0, 0.0).astype(bf16)
        for part in parts:
            got = mul(part, hot, TN)[c * half : c * half + width]
            total = got if total is None else total + got
    out_ref[...] = total


def factor_block(mat_ref, off, inv_ref, d_ref, e_ref, head_ref):
    d_ref[...] = mat_ref[pl.ds(off, BLOCK), pl.ds(off, BLOCK)]
    e_ref[...] = jnp.where(
        lax.broadcasted_iota(jnp.int32, (BLOCK, BLOCK), 0)
        == lax.broadcasted_iota(jnp.int32, (BLOCK, BLOCK), 1),
        1.0,
        0.0,
    ).astype(f32)
    full = (PANEL, BLOCK)

    def spread(a, lane):
        return jnp.broadcast_to(a[:, lane : lane + 1], full)

    for p in range(BLOCK // PANEL):
        first = p * PANEL
        rows = [jnp.broadcast_to(d_ref[first + k : first + k + 1, :], full) for k in range(PANEL)]
        invs = [jnp.broadcast_to(e_ref[first + k : first + k + 1, :], full) for k in range(PANEL)]
        lead = d_ref[first : first + PANEL, :]
        for k in range(PANEL):
            head_ref[k * PANEL : (k + 1) * PANEL, :] = spread(lead, first + k)
        s = [
            [
                jnp.broadcast_to(head_ref[k * PANEL + i : k * PANEL + i + 1, :], full)
                for k in range(i + 1)
            ]
            for i in range(PANEL)
        ]
        scale = []
        for k in range(PANEL):
            r = lax.rsqrt(s[k][k])
            scale.append(r)
            for i in range(k + 1, PANEL):
                s[i][k] = s[i][k] * r
            for i in range(k + 1, PANEL):
                for j in range(k + 1, i + 1):
                    s[i][j] = s[i][j] - s[i][k] * s[j][k]
        for k in range(PANEL):
            for m in range(k):
                rows[k] = rows[k] - s[k][m] * rows[m]
                invs[k] = invs[k] - s[k][m] * invs[m]
            rows[k] = rows[k] * scale[k]
            invs[k] = invs[k] * scale[k]
            inv_ref[first + k : first + k + 1, :] = invs[k][0:1, :]
        for b in range(p + 1, BLOCK // PANEL):
            at = slice(b * PANEL, (b + 1) * PANEL)
            d = d_ref[at, :]
            e = e_ref[at, :]
            cols = [spread(d, first + k) for k in range(PANEL)]
            for k in range(PANEL):
                for m in range(k):
                    cols[k] = cols[k] - s[k][m] * cols[m]
                cols[k] = cols[k] * scale[k]
            for k in range(PANEL):
                d = d - cols[k] * rows[k]
                e = e - cols[k] * invs[k]
            d_ref[at, :] = d
            e_ref[at, :] = e


def load_half(src_ref, emb_part, ch_ref, cl_ref):
    half, count = src_ref.shape
    sq = jnp.zeros((1, count), f32)
    for r in range(0, half, BLOCK):
        a = src_ref[r : r + BLOCK, :]
        ch_ref[r : r + BLOCK, :], cl_ref[r : r + BLOCK, :] = split2(a)
        if r < emb_part:
            sq = sq + jnp.sum(a * a, axis=0, keepdims=True)
    return sq


def products(which, emb_ref, fac_ref, ch_ref, cl_ref, emit):
    half, count = ch_ref.shape
    emb_part, fac_part = emb_ref.shape[1] // 2, fac_ref.shape[1] // 2

    def wide(lo, hi, need):
        return ch_ref[lo:hi, :need], cl_ref[lo:hi, :need]

    for i in range(count // BLOCK):
        at = slice(i * BLOCK, (i + 1) * BLOCK)
        need = (i // 2 + 1) * 2 * BLOCK
        cross = mul3((ch_ref[:emb_part, at], cl_ref[:emb_part, at]), wide(0, emb_part, need), TN)
        old = mul3((ch_ref[emb_part:, at], cl_ref[emb_part:, at]), wide(emb_part, half, need), TN)
        emit(i * BLOCK, need, cross, old)
    emb_at = pl.ds(pl.multiple_of(which * emb_part, BLOCK), emb_part)
    fac_at = pl.ds(pl.multiple_of(which * fac_part, BLOCK), fac_part)
    for r in range(0, emb_ref.shape[0], BLOCK):
        cross = mul3(split2(emb_ref[r : r + BLOCK, emb_at]), wide(0, emb_part, count), NN)
        old = mul3(split2(fac_ref[r : r + BLOCK, fac_at]), wide(emb_part, half, count), NN)
        emit(count + r, count, cross, old)


def first_kernel(core_ref, emb_ref, fac_ref, own_ref, cross_ref, old_ref, sq_ref, ch_ref, cl_ref):
    sq = load_half(own_ref, emb_ref.shape[1] // 2, ch_ref, cl_ref)
    sq_ref[...] = jnp.broadcast_to(sq, sq_ref.shape)

    def emit(row, need, cross, old):
        cross_ref[row : row + BLOCK, :need] = cross
        old_ref[row : row + BLOCK, :need] = old

    products(core_ref[0], emb_ref, fac_ref, ch_ref, cl_ref, emit)


def main_kernel(
    core_ref, emb_ref, fac_ref, other_ref, cross_ref, old_ref, own_sq_ref,
    new_ref, keep_ref, send_ref,
    ch_ref, cl_ref, sq_ref, mat_ref, inv_ref, d_ref, e_ref, head_ref, sum_ref,
):
    core = core_ref[0]
    rows_dev, width = emb_ref.shape
    old_rank = fac_ref.shape[1]
    count = other_ref.shape[1]
    scale = 1.0 / (2.0 * width)
    sq = own_sq_ref[0:1, :] + load_half(other_ref, width // 2, ch_ref, cl_ref)
    sq_ref[...] = jnp.transpose(jnp.broadcast_to(sq, (BLOCK, count)))

    def emit(row, need, cross, old):
        at = slice(row, row + BLOCK)
        cross = cross_ref[at, :need] + cross
        old = old_ref[at, :need] + old
        if row < count:
            left = sq_ref[at, 0:1]
        else:
            a = emb_ref[row - count : row - count + BLOCK, :]
            left = jnp.sum(a * a, axis=1, keepdims=True)
        block = jnp.exp((2.0 * cross - (left + sq[:, :need])) * scale) - old
        if row < count:
            r = lax.broadcasted_iota(jnp.int32, (BLOCK, need), 0) + row
            c = lax.broadcasted_iota(jnp.int32, (BLOCK, need), 1)
            block = block + jnp.where(r == c, ridge_term, 0.0)
        mat_ref[at, :need] = block

    products(1 - core, emb_ref, fac_ref, ch_ref, cl_ref, emit)

    all_rows = count + rows_dev

    def step(kb, carry):
        off = pl.multiple_of(kb * BLOCK, BLOCK)
        factor_block(mat_ref, off, inv_ref, d_ref, e_ref, head_ref)
        panel = mul3(split2(mat_ref[:, pl.ds(off, BLOCK)]), split2(inv_ref[...]), NT)
        new_ref[:, pl.ds(off, BLOCK)] = panel[count:]
        row = lax.broadcasted_iota(jnp.int32, (all_rows, BLOCK), 0)
        panel = jnp.where(row >= off + BLOCK, panel, 0.0)
        high, low = split2(panel)
        for r in range(0, all_rows, 256):
            for c in range(0, min(r + 256, count), 256):

                @pl.when(off + BLOCK < min(r, c) + 256)
                def _():
                    mat_ref[r : r + 256, c : c + 256] = mat_ref[r : r + 256, c : c + 256] - mul3(
                        (high[r : r + 256], low[r : r + 256]), (high[c : c + 256], low[c : c + 256]), NT
                    )

        return carry

    lax.fori_loop(0, count // BLOCK, step, 0)

    new = split2(new_ref[...])
    for i in range(old_rank // BLOCK):
        at = slice(i * BLOCK, (i + 1) * BLOCK)
        sum_ref[at, :] = mul3(split2(fac_ref[:, at]), new, TN)
    for i in range(count // BLOCK):
        at = slice(i * BLOCK, (i + 1) * BLOCK)
        sum_ref[old_rank + i * BLOCK : old_rank + (i + 1) * BLOCK, :] = mul3(
            (new[0][:, at], new[1][:, at]), new, TN
        )
    _, n_zh, part, _ = keep_ref.shape
    shares = keep_ref.shape[0]
    for zh in range(n_zh):
        for j in range(shares):
            start = (zh * shares + j) * 2 * part
            keep_ref[j, zh] = sum_ref[pl.ds(pl.multiple_of(start + core * part, part), part), :]
            send_ref[j, zh] = sum_ref[pl.ds(pl.multiple_of(start + (1 - core) * part, part), part), :]


VMEM = pl.BlockSpec(memory_space=pltpu.VMEM)
SMEM = pl.BlockSpec(memory_space=pltpu.SMEM)
HBM = pl.BlockSpec(memory_space=pltpu.HBM)
PARAMS = pltpu.CompilerParams(vmem_limit_bytes=24 * 1024 * 1024)
WIDE_PARAMS = pltpu.CompilerParams(vmem_limit_bytes=60 * 1024 * 1024)


def on_device(n_xy, n_z, embeddings, factor, pivots):
    rows_dev, width = embeddings.shape
    old_rank = factor.shape[1]
    count = pivots.shape[0]
    total = width + old_rank
    slices = 2 * n_xy
    piece = total // slices
    core = lax.axis_index("core")
    mine = lax.axis_index(("zl", "core", "zh", "x", "y"))
    base_place = (mine * rows_dev).astype(jnp.int32).reshape(1)
    core_place = core.astype(jnp.int32).reshape(1)
    sent = pl.pallas_call(
        functools.partial(pick_kernel, piece),
        out_shape=jax.ShapeDtypeStruct((slices, 4, BLOCK), f32),
        in_specs=[SMEM, SMEM, HBM, HBM, HBM],
        out_specs=VMEM,
        scratch_shapes=[
            pltpu.VMEM((1, count), jnp.int32),
            pltpu.VMEM((rows_dev, width), f32),
            pltpu.VMEM((rows_dev, old_rank), f32),
            pltpu.SemaphoreType.DMA((3,)),
        ],
        compiler_params=WIDE_PARAMS,
        name="pick",
    )(base_place, core_place, pivots.reshape(1, count), embeddings, factor)
    got = lax.all_to_all(sent, ("core", "x", "y"), 0, 0, tiled=True)
    packed = (got[:n_xy] + got[n_xy:])[:, :SLOTS].reshape(n_xy * SLOTS, BLOCK)
    packed = jnp.broadcast_to(packed[None], (n_z, n_xy * SLOTS, BLOCK))
    slots = lax.all_to_all(packed, ("zl", "zh"), 0, 0, tiled=True)
    chosen_slice = pl.pallas_call(
        functools.partial(select_kernel, piece),
        out_shape=jax.ShapeDtypeStruct((piece, count), f32),
        in_specs=[VMEM],
        out_specs=VMEM,
        compiler_params=PARAMS,
        name="select",
    )(slots.reshape(n_z * n_xy * SLOTS, BLOCK))
    wide = jnp.broadcast_to(chosen_slice[None], (n_xy, piece, count))
    own = lax.all_to_all(wide, ("x", "y"), 0, 0, tiled=True).reshape(n_xy * piece, count)
    other = lax.ppermute(own, "core", [(0, 1), (1, 0)])
    half = total // 2
    all_rows = count + rows_dev
    halves = [pltpu.VMEM((half, count), bf16), pltpu.VMEM((half, count), bf16)]
    table = jax.ShapeDtypeStruct((all_rows, count), f32)
    cross, old, own_sq = pl.pallas_call(
        first_kernel,
        out_shape=(table, table, jax.ShapeDtypeStruct((8, count), f32)),
        in_specs=[SMEM, VMEM, VMEM, VMEM],
        out_specs=(VMEM, VMEM, VMEM),
        scratch_shapes=halves,
        compiler_params=PARAMS,
        cost_estimate=pl.CostEstimate(
            flops=6 * half * count * all_rows, bytes_accessed=4 * half * count, transcendentals=0
        ),
        name="first",
    )(core_place, embeddings, factor, own)
    share = (old_rank + count) // slices
    part = share // 2
    split = jax.ShapeDtypeStruct((n_xy, 2, part, count), f32)
    new_factor, keep, send = pl.pallas_call(
        main_kernel,
        out_shape=(jax.ShapeDtypeStruct((rows_dev, count), f32), split, split),
        in_specs=[SMEM] + [VMEM] * 6,
        out_specs=(VMEM, VMEM, VMEM),
        scratch_shapes=halves + [
            pltpu.VMEM((count, BLOCK), f32),
            pltpu.VMEM((count + rows_dev, count), f32),
            pltpu.VMEM((BLOCK, BLOCK), f32),
            pltpu.VMEM((BLOCK, BLOCK), f32),
            pltpu.VMEM((BLOCK, BLOCK), f32),
            pltpu.VMEM((PANEL * PANEL, BLOCK), f32),
            pltpu.VMEM((old_rank + count, count), f32),
        ],
        compiler_params=PARAMS,
        name="main",
    )(core_place, embeddings, factor, other, cross, old, own_sq)
    pair = keep + lax.ppermute(send, "core", [(0, 1), (1, 0)])
    layer = jnp.sum(lax.all_to_all(pair, ("x", "y"), 0, 0, tiled=True), axis=0)
    n_zl = n_z // 2
    few = part // n_zl
    spread = jnp.swapaxes(layer.reshape(2, n_zl, few, count), 0, 1).reshape(n_z, few, count)
    summed = jnp.sum(lax.all_to_all(spread, ("zl", "zh"), 0, 0, tiled=True), axis=0)
    my_dev = lax.axis_index(("zh", "x", "y"))
    first = my_dev * share + core * part + lax.axis_index("zl") * few
    diagonal_hit = first + jnp.arange(few)[:, None] - old_rank == jnp.arange(count)[None, :]
    summed = summed + core_ridge * diagonal_hit.astype(f32)
    line = jnp.broadcast_to(summed[None], (n_zl, few, count))
    line = lax.all_to_all(line, "zl", 0, 0, tiled=True).reshape(part, count)
    return new_factor, lax.all_gather(line, "core", axis=0, tiled=True)


def solution(mesh):
    n_zl, n_zh, n_x = 8, 2, 4
    n_y = mesh.shape["dev"] // (n_zh * n_x)
    n_core = mesh.shape["grp"] // n_zl
    axes = ("zl", "core", "zh", "x", "y")
    fine = Mesh(mesh.devices.reshape(n_zl, n_core, n_zh, n_x, n_y), axes)
    in_specs = (P(axes, None), P(axes, None), P())
    out_specs = (P(axes, None), P(("zh", "x", "y"), None))
    return jax.shard_map(
        functools.partial(on_device, n_x * n_y, n_zl * n_zh),
        mesh=fine, in_specs=in_specs, out_specs=out_specs, check_vma=False,
    )
```

```python
import functools

import jax
import jax.numpy as jnp
from jax import lax
from jax.experimental import pallas as pl
from jax.experimental.pallas import tpu as pltpu
from jax.sharding import Mesh
from jax.sharding import PartitionSpec as P

ridge_term = 1.0
core_ridge = 1.0

SLOTS = 3
BLOCK = 128
PANEL = 8
f32 = jnp.float32
bf16 = jnp.bfloat16


def split2(a):
    high = a.astype(bf16)
    return high, (a - high.astype(f32)).astype(bf16)


def split3(a):
    high = a.astype(bf16)
    rest = a - high.astype(f32)
    mid = rest.astype(bf16)
    return high, mid, (rest - mid.astype(f32)).astype(bf16)


def mul(a, b, dims):
    return lax.dot_general(a, b, (dims, ((), ())), preferred_element_type=f32)


def mul3(a, b, dims):
    (ah, al), (bh, bl) = a, b
    return mul(ah, bh, dims) + (mul(ah, bl, dims) + mul(al, bh, dims))


NN = ((1,), (0,))
NT = ((1,), (1,))
TN = ((0,), (0,))


def pick_kernel(
    width, base_ref, core_ref, pivots_hbm, emb_hbm, fac_hbm, out_ref, pivots_ref, emb_ref, fac_ref, sems
):
    copies = [
        pltpu.make_async_copy(src, dst, sems.at[i])
        for i, (src, dst) in enumerate(
            ((pivots_hbm, pivots_ref), (emb_hbm, emb_ref), (fac_hbm, fac_ref))
        )
    ]
    for copy in copies:
        copy.start()
    copies[0].wait()
    base, core = base_ref[0], core_ref[0]
    rows_dev = emb_ref.shape[0]
    count = pivots_ref.shape[1]
    local = (pivots_ref[...] - base).astype(f32)
    order = lax.broadcasted_iota(jnp.int32, (1, count), 1).astype(f32)
    inside = jnp.where((local >= 0) & (local < rows_dev), 1.0, 0.0)
    sub = lax.broadcasted_iota(jnp.int32, (8, rows_dev), 0)
    lane = lax.broadcasted_iota(jnp.int32, (8, rows_dev), 1).astype(f32)
    sub_tag = lax.broadcasted_iota(jnp.int32, (8, BLOCK), 0)
    hot = jnp.zeros((8, rows_dev), f32)
    tag = jnp.full((8, BLOCK), -1.0, f32)
    for k in range(SLOTS):
        pos = jnp.min(jnp.where(inside > 0, order, float(count)), axis=1, keepdims=True)
        hit = order == pos
        row = jnp.sum(jnp.where(hit, local, 0.0), axis=1, keepdims=True)
        valid = pos < count
        row = jnp.where(valid, row, -1.0)
        hot = hot + jnp.where((sub == k) & (lane == row), 1.0, 0.0)
        tag = jnp.where((sub_tag == k), jnp.where(valid, pos, -1.0), tag)
        inside = jnp.where(hit, 0.0, inside)
    hot = hot.astype(bf16)
    copies[1].wait()
    copies[2].wait()
    pieces = []
    for h in range(2):
        for ref in (emb_ref, fac_ref):
            step = ref.shape[1] // 2
            high, mid, low = split3(ref[:, h * step : (h + 1) * step])
            pieces.append(mul(hot, high, NN) + (mul(hot, mid, NN) + mul(hot, low, NN)))
    rows = jnp.concatenate(pieces + [jnp.zeros((8, BLOCK), f32)], axis=1)
    lane_out = lax.broadcasted_iota(jnp.int32, (8, BLOCK), 1)
    for j in range(out_ref.shape[0]):
        first = width * j
        tile = first // BLOCK * BLOCK
        window = rows[:, tile : tile + 2 * BLOCK]
        if first > tile:
            window = pltpu.roll(window, 2 * BLOCK - (first - tile), 1)
        piece = jnp.where(lane_out < width, window[:, :BLOCK], jnp.where(lane_out == width, tag, 0.0))
        piece = jnp.where(core == 0, piece, pltpu.roll(piece, BLOCK // 2, 1))
        out_ref[j] = piece[:4]


def select_kernel(width, slots_ref, out_ref):
    slots = slots_ref[...]
    count = out_ref.shape[1]
    order = lax.broadcasted_iota(jnp.int32, (1, count), 1).astype(f32)
    half = BLOCK // 2
    parts = split3(slots)
    total = None
    for c in range(2):
        tag = slots[:, c * half + width : c * half + width + 1]
        hot = jnp.where(tag == order, 1.0, 0.0).astype(bf16)
        for part in parts:
            got = mul(part, hot, TN)[c * half : c * half + width]
            total = got if total is None else total + got
    out_ref[...] = total


def factor_block(mat_ref, off, inv_ref, d_ref, e_ref, head_ref):
    d_ref[...] = mat_ref[pl.ds(off, BLOCK), pl.ds(off, BLOCK)]
    e_ref[...] = jnp.where(
        lax.broadcasted_iota(jnp.int32, (BLOCK, BLOCK), 0)
        == lax.broadcasted_iota(jnp.int32, (BLOCK, BLOCK), 1),
        1.0,
        0.0,
    ).astype(f32)
    full = (PANEL, BLOCK)

    def spread(a, lane):
        return jnp.broadcast_to(a[:, lane : lane + 1], full)

    for p in range(BLOCK // PANEL):
        first = p * PANEL
        rows = [jnp.broadcast_to(d_ref[first + k : first + k + 1, :], full) for k in range(PANEL)]
        invs = [jnp.broadcast_to(e_ref[first + k : first + k + 1, :], full) for k in range(PANEL)]
        lead = d_ref[first : first + PANEL, :]
        for k in range(PANEL):
            head_ref[k * PANEL : (k + 1) * PANEL, :] = spread(lead, first + k)
        s = [
            [
                jnp.broadcast_to(head_ref[k * PANEL + i : k * PANEL + i + 1, :], full)
                for k in range(i + 1)
            ]
            for i in range(PANEL)
        ]
        scale = []
        for k in range(PANEL):
            r = lax.rsqrt(s[k][k])
            scale.append(r)
            for i in range(k + 1, PANEL):
                s[i][k] = s[i][k] * r
            for i in range(k + 1, PANEL):
                for j in range(k + 1, i + 1):
                    s[i][j] = s[i][j] - s[i][k] * s[j][k]
        for k in range(PANEL):
            for m in range(k):
                rows[k] = rows[k] - s[k][m] * rows[m]
                invs[k] = invs[k] - s[k][m] * invs[m]
            rows[k] = rows[k] * scale[k]
            invs[k] = invs[k] * scale[k]
            inv_ref[first + k : first + k + 1, :] = invs[k][0:1, :]
        for b in range(p + 1, BLOCK // PANEL):
            at = slice(b * PANEL, (b + 1) * PANEL)
            d = d_ref[at, :]
            e = e_ref[at, :]
            cols = [spread(d, first + k) for k in range(PANEL)]
            for k in range(PANEL):
                for m in range(k):
                    cols[k] = cols[k] - s[k][m] * cols[m]
                cols[k] = cols[k] * scale[k]
            for k in range(PANEL):
                d = d - cols[k] * rows[k]
                e = e - cols[k] * invs[k]
            d_ref[at, :] = d
            e_ref[at, :] = e


def load_half(src_ref, emb_part, ch_ref, cl_ref):
    half, count = src_ref.shape
    sq = jnp.zeros((1, count), f32)
    for r in range(0, half, BLOCK):
        a = src_ref[r : r + BLOCK, :]
        ch_ref[r : r + BLOCK, :], cl_ref[r : r + BLOCK, :] = split2(a)
        if r < emb_part:
            sq = sq + jnp.sum(a * a, axis=0, keepdims=True)
    return sq


def products(which, emb_ref, fac_ref, ch_ref, cl_ref, emit):
    half, count = ch_ref.shape
    emb_part, fac_part = emb_ref.shape[1] // 2, fac_ref.shape[1] // 2

    def wide(lo, hi, need):
        return ch_ref[lo:hi, :need], cl_ref[lo:hi, :need]

    for i in range(count // BLOCK):
        at = slice(i * BLOCK, (i + 1) * BLOCK)
        need = (i // 2 + 1) * 2 * BLOCK
        cross = mul3((ch_ref[:emb_part, at], cl_ref[:emb_part, at]), wide(0, emb_part, need), TN)
        old = mul3((ch_ref[emb_part:, at], cl_ref[emb_part:, at]), wide(emb_part, half, need), TN)
        emit(i * BLOCK, need, cross, old)
    emb_at = pl.ds(pl.multiple_of(which * emb_part, BLOCK), emb_part)
    fac_at = pl.ds(pl.multiple_of(which * fac_part, BLOCK), fac_part)
    for r in range(0, emb_ref.shape[0], BLOCK):
        cross = mul3(split2(emb_ref[r : r + BLOCK, emb_at]), wide(0, emb_part, count), NN)
        old = mul3(split2(fac_ref[r : r + BLOCK, fac_at]), wide(emb_part, half, count), NN)
        emit(count + r, count, cross, old)


def first_kernel(core_ref, emb_ref, fac_ref, own_ref, cross_ref, old_ref, sq_ref, ch_ref, cl_ref):
    sq = load_half(own_ref, emb_ref.shape[1] // 2, ch_ref, cl_ref)
    sq_ref[...] = jnp.broadcast_to(sq, sq_ref.shape)

    def emit(row, need, cross, old):
        cross_ref[row : row + BLOCK, :need] = cross
        old_ref[row : row + BLOCK, :need] = old

    products(core_ref[0], emb_ref, fac_ref, ch_ref, cl_ref, emit)


def main_kernel(
    core_ref, emb_ref, fac_ref, other_ref, cross_ref, old_ref, own_sq_ref,
    new_ref, keep_ref, send_ref,
    ch_ref, cl_ref, sq_ref, mat_ref, inv_ref, d_ref, e_ref, head_ref, sum_ref,
):
    core = core_ref[0]
    rows_dev, width = emb_ref.shape
    old_rank = fac_ref.shape[1]
    count = other_ref.shape[1]
    scale = 1.0 / (2.0 * width)
    sq = own_sq_ref[0:1, :] + load_half(other_ref, width // 2, ch_ref, cl_ref)
    sq_ref[...] = jnp.transpose(jnp.broadcast_to(sq, (BLOCK, count)))

    def emit(row, need, cross, old):
        at = slice(row, row + BLOCK)
        cross = cross_ref[at, :need] + cross
        old = old_ref[at, :need] + old
        if row < count:
            left = sq_ref[at, 0:1]
        else:
            a = emb_ref[row - count : row - count + BLOCK, :]
            left = jnp.sum(a * a, axis=1, keepdims=True)
        block = jnp.exp((2.0 * cross - (left + sq[:, :need])) * scale) - old
        if row < count:
            r = lax.broadcasted_iota(jnp.int32, (BLOCK, need), 0) + row
            c = lax.broadcasted_iota(jnp.int32, (BLOCK, need), 1)
            block = block + jnp.where(r == c, ridge_term, 0.0)
        mat_ref[at, :need] = block

    products(1 - core, emb_ref, fac_ref, ch_ref, cl_ref, emit)

    all_rows = count + rows_dev

    def step(kb, carry):
        off = pl.multiple_of(kb * BLOCK, BLOCK)
        factor_block(mat_ref, off, inv_ref, d_ref, e_ref, head_ref)
        ah, al = split2(mat_ref[:, pl.ds(off, BLOCK)])
        bh, bl = split2(inv_ref[...])
        panel = mul(jnp.concatenate([ah, ah, al], axis=1), jnp.concatenate([bh, bl, bh], axis=1), NT)
        new_ref[:, pl.ds(off, BLOCK)] = panel[count:]
        row = lax.broadcasted_iota(jnp.int32, (all_rows, BLOCK), 0)
        panel = jnp.where(row >= off + BLOCK, panel, 0.0)
        high, low = split2(panel)
        left = jnp.concatenate([high, high, low], axis=1)
        right = jnp.concatenate([high[:count], low[:count], high[:count]], axis=1)
        for r in range(0, all_rows, 256):
            for c in range(0, min(r + 256, count), 256):

                @pl.when(off + BLOCK < min(r, c) + 256)
                def _():
                    mat_ref[r : r + 256, c : c + 256] = mat_ref[r : r + 256, c : c + 256] - mul(
                        left[r : r + 256], right[c : c + 256], NT
                    )

        return carry

    lax.fori_loop(0, count // BLOCK, step, 0)

    new = split2(new_ref[...])
    for i in range(old_rank // BLOCK):
        at = slice(i * BLOCK, (i + 1) * BLOCK)
        sum_ref[at, :] = mul3(split2(fac_ref[:, at]), new, TN)
    for i in range(count // BLOCK):
        at = slice(i * BLOCK, (i + 1) * BLOCK)
        sum_ref[old_rank + i * BLOCK : old_rank + (i + 1) * BLOCK, :] = mul3(
            (new[0][:, at], new[1][:, at]), new, TN
        )
    _, n_zh, part, _ = keep_ref.shape
    shares = keep_ref.shape[0]
    for zh in range(n_zh):
        for j in range(shares):
            start = (zh * shares + j) * 2 * part
            keep_ref[j, zh] = sum_ref[pl.ds(pl.multiple_of(start + core * part, part), part), :]
            send_ref[j, zh] = sum_ref[pl.ds(pl.multiple_of(start + (1 - core) * part, part), part), :]


def layer_kernel(parts_ref, out_ref):
    few = out_ref.shape[1]
    n_zh = parts_ref.shape[1]
    for zh in range(n_zh):
        total = jnp.sum(parts_ref[:, zh], axis=0)
        for zl in range(out_ref.shape[0] // n_zh):
            out_ref[zl * n_zh + zh] = total[zl * few : (zl + 1) * few]


VMEM = pl.BlockSpec(memory_space=pltpu.VMEM)
SMEM = pl.BlockSpec(memory_space=pltpu.SMEM)
HBM = pl.BlockSpec(memory_space=pltpu.HBM)
PARAMS = pltpu.CompilerParams(vmem_limit_bytes=24 * 1024 * 1024)
WIDE_PARAMS = pltpu.CompilerParams(vmem_limit_bytes=60 * 1024 * 1024)


def on_device(n_xy, n_z, embeddings, factor, pivots):
    rows_dev, width = embeddings.shape
    old_rank = factor.shape[1]
    count = pivots.shape[0]
    total = width + old_rank
    slices = 2 * n_xy
    piece = total // slices
    core = lax.axis_index("core")
    mine = lax.axis_index(("zl", "core", "zh", "x", "y"))
    base_place = (mine * rows_dev).astype(jnp.int32).reshape(1)
    core_place = core.astype(jnp.int32).reshape(1)
    sent = pl.pallas_call(
        functools.partial(pick_kernel, piece),
        out_shape=jax.ShapeDtypeStruct((slices, 4, BLOCK), f32),
        in_specs=[SMEM, SMEM, HBM, HBM, HBM],
        out_specs=VMEM,
        scratch_shapes=[
            pltpu.VMEM((1, count), jnp.int32),
            pltpu.VMEM((rows_dev, width), f32),
            pltpu.VMEM((rows_dev, old_rank), f32),
            pltpu.SemaphoreType.DMA((3,)),
        ],
        compiler_params=WIDE_PARAMS,
        name="pick",
    )(base_place, core_place, pivots.reshape(1, count), embeddings, factor)
    got = lax.all_to_all(sent, ("core", "x", "y"), 0, 0, tiled=True)
    packed = (got[:n_xy] + got[n_xy:])[:, :SLOTS].reshape(n_xy * SLOTS, BLOCK)
    packed = jnp.broadcast_to(packed[None], (n_z, n_xy * SLOTS, BLOCK))
    slots = lax.all_to_all(packed, ("zl", "zh"), 0, 0, tiled=True)
    chosen_slice = pl.pallas_call(
        functools.partial(select_kernel, piece),
        out_shape=jax.ShapeDtypeStruct((piece, count), f32),
        in_specs=[VMEM],
        out_specs=VMEM,
        compiler_params=PARAMS,
        name="select",
    )(slots.reshape(n_z * n_xy * SLOTS, BLOCK))
    wide = jnp.broadcast_to(chosen_slice[None], (n_xy, piece, count))
    own = lax.all_to_all(wide, ("x", "y"), 0, 0, tiled=True).reshape(n_xy * piece, count)
    other = lax.ppermute(own, "core", [(0, 1), (1, 0)])
    half = total // 2
    all_rows = count + rows_dev
    halves = [pltpu.VMEM((half, count), bf16), pltpu.VMEM((half, count), bf16)]
    table = jax.ShapeDtypeStruct((all_rows, count), f32)
    cross, old, own_sq = pl.pallas_call(
        first_kernel,
        out_shape=(table, table, jax.ShapeDtypeStruct((8, count), f32)),
        in_specs=[SMEM, VMEM, VMEM, VMEM],
        out_specs=(VMEM, VMEM, VMEM),
        scratch_shapes=halves,
        compiler_params=PARAMS,
        cost_estimate=pl.CostEstimate(
            flops=6 * half * count * all_rows, bytes_accessed=4 * half * count, transcendentals=0
        ),
        name="first",
    )(core_place, embeddings, factor, own)
    share = (old_rank + count) // slices
    part = share // 2
    split = jax.ShapeDtypeStruct((n_xy, 2, part, count), f32)
    new_factor, keep, send = pl.pallas_call(
        main_kernel,
        out_shape=(jax.ShapeDtypeStruct((rows_dev, count), f32), split, split),
        in_specs=[SMEM] + [VMEM] * 6,
        out_specs=(VMEM, VMEM, VMEM),
        scratch_shapes=halves + [
            pltpu.VMEM((count, BLOCK), f32),
            pltpu.VMEM((count + rows_dev, count), f32),
            pltpu.VMEM((BLOCK, BLOCK), f32),
            pltpu.VMEM((BLOCK, BLOCK), f32),
            pltpu.VMEM((BLOCK, BLOCK), f32),
            pltpu.VMEM((PANEL * PANEL, BLOCK), f32),
            pltpu.VMEM((old_rank + count, count), f32),
        ],
        compiler_params=PARAMS,
        name="main",
    )(core_place, embeddings, factor, other, cross, old, own_sq)
    pair = keep + lax.ppermute(send, "core", [(0, 1), (1, 0)])
    parts = lax.all_to_all(pair, ("x", "y"), 0, 0, tiled=True)
    n_zl = n_z // 2
    few = part // n_zl
    spread = pl.pallas_call(
        layer_kernel,
        out_shape=jax.ShapeDtypeStruct((n_z, few, count), f32),
        in_specs=[VMEM],
        out_specs=VMEM,
        compiler_params=PARAMS,
        name="layer",
    )(parts)
    summed = jnp.sum(lax.all_to_all(spread, ("zl", "zh"), 0, 0, tiled=True), axis=0)
    my_dev = lax.axis_index(("zh", "x", "y"))
    first = my_dev * share + core * part + lax.axis_index("zl") * few
    diagonal_hit = first + jnp.arange(few)[:, None] - old_rank == jnp.arange(count)[None, :]
    summed = summed + core_ridge * diagonal_hit.astype(f32)
    line = jnp.broadcast_to(summed[None], (n_zl, few, count))
    line = lax.all_to_all(line, "zl", 0, 0, tiled=True).reshape(part, count)
    return new_factor, lax.all_gather(line, "core", axis=0, tiled=True)


def solution(mesh):
    n_zl, n_zh, n_x = 8, 2, 4
    n_y = mesh.shape["dev"] // (n_zh * n_x)
    n_core = mesh.shape["grp"] // n_zl
    axes = ("zl", "core", "zh", "x", "y")
    fine = Mesh(mesh.devices.reshape(n_zl, n_core, n_zh, n_x, n_y), axes)
    in_specs = (P(axes, None), P(axes, None), P())
    out_specs = (P(axes, None), P(("zh", "x", "y"), None))
    return jax.shard_map(
        functools.partial(on_device, n_x * n_y, n_zl * n_zh),
        mesh=fine, in_specs=in_specs, out_specs=out_specs, check_vma=False,
    )
```
